32 devices in a mesh: prompt: 4 (over x, core), resp: 8 (over z, y).
Axes of the slice: x: 2, y: 2, z: 4, core: 2. Of those that a mesh axis runs over, the one named last changes fastest.
Arguments:
- queries: bfloat16 [32, 256, 4096], P(('prompt', 'resp')), may hold values from -5 to 5
- resp_keys: bfloat16 [32, 256, 512], P(('prompt', 'resp')), may hold values from -6 to 6
- resp_values: bfloat16 [32, 256, 512], P(('prompt', 'resp')), may hold values from -6 to 6
- grad_out: bfloat16 [32, 256, 4096], P(('prompt', 'resp')), may hold values from -24 to 24
- prompt_keys: bfloat16 [4, 256, 512], P('prompt', 'resp'), may hold values from -5 to 5
- prompt_values: bfloat16 [4, 256, 512], P('prompt', 'resp'), may hold values from -6 to 6
- group_sizes: int32 [4], replicated, may hold values from 1 to 16, 32 in all
- slot_response: int32 [32], replicated, may hold values from 0 to 31, each once
- lengths: int32 [32], P(('prompt', 'resp')), may hold values from 1 to 256, as said below
Outputs:
- grad_queries: bfloat16 [32, 256, 4096], P(('prompt', 'resp'))
- grad_resp_keys: bfloat16 [32, 256, 512], P(('prompt', 'resp'))
- grad_resp_values: bfloat16 [32, 256, 512], P(('prompt', 'resp'))
- grad_prompt_keys: float32 [4, 256, 512], P('prompt', 'resp')
- grad_prompt_values: float32 [4, 256, 512], P('prompt', 'resp')
The draws below stay inside these ranges and needn't reach their ends.
Inputs may be any that keep to these rules, and one draw needn't show every extreme that they name: `group_sizes`: group sizes sum to 32; a group may hold a single response; the largest is exactly 16. `slot_response`: each response appears in exactly one slot. `lengths`: some response block is full.
All inputs are finite; a program needn't handle non-finite values.
Results may differ from the reference program's by a relative error of at most 0.012.
Values may be sent and summed in bfloat16 or wider, within the bound.
A program may use at most 128 MiB of HBM per device.

```python
import math
import jax
import jax.numpy as jnp
import numpy as np
from jax import lax

QH = 32
KVH = 4
HD = 128
TOK = 256
PL = 256
GRP = 8
QW = 4096
KVW = 512
NPROMPT = 4
RESP = 32
GMOST = 16


def draw_queries(key, part):
    key = jax.random.fold_in(key, 11)
    base = jnp.clip(jax.random.normal(key, (RESP, TOK, QW), jnp.float32), -5.0, 5.0)
    return base.astype(jnp.bfloat16)


def draw_prompt_keys(key, part):
    key = jax.random.fold_in(key, 12)
    base = jnp.clip(jax.random.normal(key, (NPROMPT, PL, KVW), jnp.float32), -5.0, 5.0)
    return base.astype(jnp.bfloat16)


def draw_lengths(key, part):
    key = jax.random.fold_in(key, 13)
    first_key, second_key = jax.random.split(key)
    values = jax.random.randint(first_key, (RESP,), 1, TOK + 1)
    full_at = jax.random.randint(second_key, (), 0, RESP)
    return jnp.where(jnp.arange(RESP) == full_at, TOK, values).astype(jnp.int32)


def levels(stream_key, extent, pieces, smallest, largest):
    factor_of = 1.0
    for dim, blocks in pieces:
        draws = jax.random.uniform(jax.random.fold_in(jax.random.fold_in(stream_key, 6), dim), (blocks,), jnp.float32, smallest / len(pieces), largest / len(pieces))
        factor_of = factor_of * jnp.repeat(jnp.exp(draws), extent[dim] // blocks).reshape((-1,) + (1,) * (len(extent) - 1 - dim))
    return factor_of


def length_profile(number_of, total, limit, slope):
    portions = [(1 << 20) // math.isqrt(standing ** slope) + 1 for standing in range(2, number_of + 1)]
    spare, holding = total - limit - (number_of - 1), [1] * (number_of - 1)
    while spare > 0:
        movable = [i for i in range(number_of - 1) if holding[i] < limit]
        whole, left = sum([portions[i] for i in movable]), spare
        for i in movable:
            addition = min(limit - holding[i], max(1, left * portions[i] // whole), spare)
            holding[i] = holding[i] + addition
            spare = spare - addition
    return np.array([limit] + holding)


def ragged(key, amount, total, bound, skew):
    if amount == 2:
        one = jax.random.randint(key, (), max(1, total - bound), min(bound, total - 1) + 1)
        return jnp.stack([one, total - one])
    sizes = jnp.asarray(length_profile(amount, total, bound, skew), jnp.int32)
    pairs = (amount - 1) // 2
    donor, sink = sizes[1:1 + 2 * pairs:2], sizes[2:2 + 2 * pairs:2]
    room = jnp.minimum(donor - 1, bound - sink)
    passed = jax.random.randint(jax.random.fold_in(key, 1), (pairs,), 0, 1 << 20) % (room + 1)
    sizes = sizes.at[1:1 + 2 * pairs:2].set(donor - passed).at[2:2 + 2 * pairs:2].set(sink + passed)
    return sizes[jax.random.permutation(jax.random.fold_in(key, 2), amount)]


def gaussian(key, shape, width, bound, shards=(), held_as=jnp.bfloat16):
    result = jax.random.normal(key, shape, jnp.float32) * width
    if len(shards) > 0:
        result = levels(key, shape, shards, -0.22, 0.18) * result
    return jnp.clip(result, min=-bound, max=bound).astype(held_as)


def setup_inputs(seed: int = 0) -> dict:
    arg_keys = jax.random.split(jax.random.key(seed), 10)
    return {
        "queries": draw_queries(jax.random.fold_in(arg_keys[9], 71), 0),
        "resp_keys": gaussian(arg_keys[1], (RESP, TOK, KVW), 1.0, 6.0, ((0, 32),)),
        "resp_values": gaussian(arg_keys[2], (RESP, TOK, KVW), 1.0, 6.0, ((0, 32),)),
        "grad_out": gaussian(arg_keys[3], (RESP, TOK, QW), 4.0, 24.0, ((0, 32),)),
        "prompt_keys": draw_prompt_keys(jax.random.fold_in(arg_keys[9], 71), 0),
        "prompt_values": gaussian(arg_keys[5], (NPROMPT, PL, KVW), 1.0, 6.0, ((0, 4), (1, 8))),
        "group_sizes": ragged(arg_keys[6], NPROMPT, RESP, GMOST, 2).astype(jnp.int32),
        "slot_response": jax.random.permutation(arg_keys[7], RESP).astype(jnp.int32),
        "lengths": draw_lengths(jax.random.fold_in(arg_keys[9], 71), 0),
    }


def per_response(query, prompt_k, prompt_v, resp_k, resp_v, upstream, length):
    tok_count = query.shape[0]
    prompt_len = prompt_k.shape[0]
    scaling = 1.0 / math.sqrt(HD)
    key_rows = jnp.concatenate([prompt_k, resp_k], 0).astype(jnp.float32).reshape(-1, KVH, HD)
    value_rows = jnp.concatenate([prompt_v, resp_v], 0).astype(jnp.float32).reshape(-1, KVH, HD)
    row_ids = jnp.arange(tok_count)[:, None]
    col_ids = jnp.arange(prompt_len + tok_count)[None, :] - prompt_len
    allowed = (col_ids < 0) | (col_ids <= row_ids) & (col_ids < length)
    live_rows = jnp.arange(tok_count) < length
    upstream = jnp.where(live_rows[:, None], upstream, jnp.zeros_like(upstream))
    query_f = query.astype(jnp.float32).reshape(tok_count, KVH, GRP, HD)
    upstream_f = upstream.astype(jnp.float32).reshape(tok_count, KVH, GRP, HD)
    scores = jnp.einsum('tkgh,jkh->kgtj', query_f, key_rows) * scaling
    scores = jnp.where(allowed[None, None], scores, -jnp.inf)
    row_max = lax.optimization_barrier(jnp.max(scores, axis=-1, keepdims=True))
    unnorm = jnp.exp(scores - row_max)
    probs = unnorm / lax.optimization_barrier(jnp.sum(unnorm, axis=-1, keepdims=True))
    probs_low = lax.optimization_barrier(probs.astype(jnp.bfloat16)).astype(jnp.float32)
    attended = jnp.einsum('kgtj,jkh->tkgh', probs_low, value_rows)
    row_dot = lax.optimization_barrier(jnp.sum(upstream_f * attended, axis=-1))
    dprob = jnp.einsum('tkgh,jkh->kgtj', upstream_f, value_rows)
    dscore = probs * (dprob - jnp.transpose(row_dot, (1, 2, 0))[..., None])
    dscore = lax.optimization_barrier(dscore.astype(jnp.bfloat16)).astype(jnp.float32)
    grad_q = jnp.einsum('kgtj,jkh->tkgh', dscore, key_rows) * scaling
    grad_k = jnp.einsum('kgtj,tkgh->jkh', dscore, query_f) * scaling
    grad_v = jnp.einsum('kgtj,tkgh->jkh', probs_low, upstream_f)
    grad_k = grad_k.reshape(prompt_len + tok_count, KVH * HD)
    grad_v = grad_v.reshape(prompt_len + tok_count, KVH * HD)
    grad_q = grad_q.reshape(tok_count, QH * HD).astype(jnp.bfloat16)
    return (grad_q, grad_k[:prompt_len], grad_v[:prompt_len], grad_k[prompt_len:].astype(jnp.bfloat16), grad_v[prompt_len:].astype(jnp.bfloat16))

def reference(queries, resp_keys, resp_values, grad_out, prompt_keys, prompt_values, group_sizes, slot_response, lengths):
    group_ends = jnp.cumsum(group_sizes)
    prompt_of = lax.optimization_barrier(jnp.sum((slot_response[:, None] >= group_ends[None, :]).astype(jnp.int32), axis=1)).astype(jnp.int32)

    def apply_one(packed):
        query, resp_k, resp_v, upstream, prompt_id, length = packed
        return per_response(query, prompt_keys[prompt_id], prompt_values[prompt_id], resp_k, resp_v, upstream, length)
    grad_q, prompt_kg, prompt_vg, resp_kg, resp_vg = lax.map(apply_one, (queries, resp_keys, resp_values, grad_out, prompt_of, lengths))
    grad_pk = jnp.zeros(prompt_keys.shape, jnp.float32).at[prompt_of].add(prompt_kg)
    grad_pv = jnp.zeros(prompt_values.shape, jnp.float32).at[prompt_of].add(prompt_vg)
    return (grad_q, resp_kg, resp_vg, grad_pk, grad_pv)
```

```python
import functools
import math

import jax
import jax.numpy as jnp
from jax import lax
from jax.experimental import pallas as pl
from jax.experimental.pallas import tpu as pltpu
from jax.sharding import PartitionSpec as P

HD = 128
GRP = 8
MESH = pl.DeviceIdType.MESH
F32 = jnp.float32
BF16 = jnp.bfloat16


def nt(a, b):
    return lax.dot_general(a, b, (((1,), (1,)), ((), ())), preferred_element_type=F32)


def nn(a, b):
    return jnp.dot(a, b, preferred_element_type=F32)


def kernel(
    n_p,
    n_r,
    q_hbm,
    do_hbm,
    rk_ref,
    rv_ref,
    pk_ref,
    pv_ref,
    sizes_ref,
    slot_ref,
    len_ref,
    gq_hbm,
    grk_ref,
    grv_ref,
    gpk_ref,
    gpv_ref,
    q_v,
    do_v,
    gq_v,
    g1,
    s2,
    r2,
    sa,
    ra,
    sb,
    rb,
    kbuf,
    vbuf,
    ktbuf,
    gk_acc,
    gv_acc,
    in_sem,
    out_sem,
    g1_send,
    g1_recv,
    s2_send,
    s2_recv,
    a_send,
    a_recv,
    b_send,
    b_recv,
):
    c = lax.axis_index("prompt")
    r = lax.axis_index("resp")
    rows = pk_ref.shape[1]
    kv_heads = pk_ref.shape[2] // HD
    tok = rk_ref.shape[1]
    plen = rows * n_r
    half = tok // 2
    top = plen + half
    scaling = 1.0 / math.sqrt(HD)
    to_exp2 = scaling * math.log2(math.e)

    def column_peer(i):
        return lax.rem(c + i, n_p)

    def row_peer(i):
        return lax.rem(r + i, n_r)

    def prompt_of(resp_index):
        value = slot_ref[c * n_r + resp_index]
        end = sizes_ref[0]
        found = (value >= end).astype(jnp.int32)
        for k in range(1, n_p - 1):
            end = end + sizes_ref[k]
            found = found + (value >= end).astype(jnp.int32)
        return found

    q_in = pltpu.make_async_copy(q_hbm.at[0], q_v, in_sem.at[0])
    do_in = pltpu.make_async_copy(do_hbm.at[0], do_v, in_sem.at[1])
    q_in.start()
    do_in.start()

    barrier = pltpu.get_barrier_semaphore()
    for i in range(1, n_p):
        pl.semaphore_signal(barrier, inc=1, device_id=(column_peer(i), r), device_id_type=MESH)
    for i in range(1, n_r):
        pl.semaphore_signal(barrier, inc=1, device_id=(c, row_peer(i)), device_id_type=MESH)
    g1[c, 0] = pk_ref[0]
    g1[c, 1] = pv_ref[0]
    pl.semaphore_wait(barrier, n_p + n_r - 2)

    def gather_first(to, slot):
        return pltpu.make_async_remote_copy(
            src_ref=g1.at[slot],
            dst_ref=g1.at[slot],
            send_sem=g1_send.at[to],
            recv_sem=g1_recv.at[slot],
            device_id=(to, r),
            device_id_type=MESH,
        )

    def gather_second(kv, to, slot):
        return pltpu.make_async_remote_copy(
            src_ref=s2.at[kv, to],
            dst_ref=r2.at[kv, slot],
            send_sem=s2_send.at[kv, to],
            recv_sem=s2_recv.at[kv, slot],
            device_id=(c, to),
            device_id_type=MESH,
        )

    def sum_first(kv, to, slot):
        return pltpu.make_async_remote_copy(
            src_ref=sa.at[kv, to],
            dst_ref=ra.at[kv, slot],
            send_sem=a_send.at[kv, to],
            recv_sem=a_recv.at[kv, slot],
            device_id=(c, to),
            device_id_type=MESH,
        )

    def sum_second(kv, to, slot):
        return pltpu.make_async_remote_copy(
            src_ref=sb.at[kv, to],
            dst_ref=rb.at[kv, slot],
            send_sem=b_send.at[kv, to],
            recv_sem=b_recv.at[kv, slot],
            device_id=(to, r),
            device_id_type=MESH,
        )

    for i in range(1, n_p):
        gather_first(column_peer(i), c).start()
    for i in range(1, n_p):
        gather_first(column_peer(i), column_peer(i)).wait_recv()
    for kv in range(kv_heads):
        lanes = slice(kv * HD, (kv + 1) * HD)
        for i in range(1, n_r):
            to = row_peer(i)
            s2[kv, to] = g1[prompt_of(to), :, :, lanes]
            gather_second(kv, to, r).start()
        r2[kv, r] = g1[prompt_of(r), :, :, lanes]

    length = len_ref[0]
    live_mask = lax.broadcasted_iota(jnp.int32, (tok, HD), 0) < length
    causal = lax.broadcasted_iota(jnp.int32, (half, half), 0) <= lax.broadcasted_iota(
        jnp.int32, (half, half), 1
    )

    def one_head(head):
        lanes = pl.ds(pl.multiple_of(head * HD, HD), HD)
        q = q_v[:, lanes]
        live = jnp.where(live_mask, do_v[:, lanes], jnp.zeros((), BF16))
        q_b = q[half:]
        live_b = live[half:]
        s_a = nt(kbuf[:top], q)
        s_b = nt(kbuf[top:], q_b)
        s_p = s_a[:plen]
        s_c0 = jnp.where(causal, s_a[plen:, :half], -jnp.inf)
        s_c = jnp.concatenate([s_c0, s_a[plen:, half:]], axis=1)
        s_b = jnp.where(causal, s_b, -jnp.inf)
        m_a = jnp.maximum(
            jnp.max(s_p, axis=0, keepdims=True), jnp.max(s_c, axis=0, keepdims=True)
        )
        m_b = jnp.maximum(m_a[:, half:], jnp.max(s_b, axis=0, keepdims=True))
        m = jnp.concatenate([m_a[:, :half], m_b], axis=1) * to_exp2
        e_p = jnp.exp2(s_p * to_exp2 - m)
        e_c = jnp.exp2(s_c * to_exp2 - m)
        e_b = jnp.exp2(s_b * to_exp2 - m[:, half:])
        d_a = nt(vbuf[:top], live)
        d_b = nt(vbuf[top:], live_b)
        d_p = d_a[:plen]
        d_c = d_a[plen:]

        def total(a, b, low):
            first = jnp.sum(a, axis=0, keepdims=True) + jnp.sum(b, axis=0, keepdims=True)
            second = first[:, half:] + jnp.sum(low, axis=0, keepdims=True)
            return jnp.concatenate([first[:, :half], second], axis=1)

        inv = 1.0 / total(e_p, e_c, e_b)
        dot_row = total(e_p * d_p, e_c * d_c, e_b * d_b) * inv
        p_p = e_p * inv
        p_c = e_c * inv
        p_b = e_b * inv[:, half:]
        ds_p = (p_p * (d_p - dot_row)).astype(BF16)
        ds_c = (p_c * (d_c - dot_row)).astype(BF16)
        ds_b = (p_b * (d_b - dot_row[:, half:])).astype(BF16)
        gk_acc[:plen] += nn(ds_p, q)
        gk_acc[plen:top] += nn(ds_c, q)
        gk_acc[top:] += nn(ds_b, q_b)
        gv_acc[:plen] += nn(p_p.astype(BF16), live)
        gv_acc[plen:top] += nn(p_c.astype(BF16), live)
        gv_acc[top:] += nn(p_b.astype(BF16), live_b)
        g_a = nn(ktbuf[:, :plen], ds_p) + nn(ktbuf[:, plen:top], ds_c)
        g_b = g_a[:, half:] + nn(ktbuf[:, top:], ds_b)
        g_t = jnp.concatenate([g_a[:, :half], g_b], axis=1) * scaling
        gq_v[:, lanes] = jnp.transpose(g_t).astype(BF16)

    def attend(kv):
        lanes = slice(kv * HD, (kv + 1) * HD)
        for i in range(1, n_r):
            gather_second(kv, row_peer(i), row_peer(i)).wait_recv()
        kbuf[:plen] = r2[kv, :, 0].reshape(plen, HD)
        vbuf[:plen] = r2[kv, :, 1].reshape(plen, HD)
        kbuf[plen:] = rk_ref[0, :, lanes]
        vbuf[plen:] = rv_ref[0, :, lanes]
        ktbuf[...] = jnp.transpose(kbuf[...].astype(F32)).astype(BF16)
        gk_acc[...] = jnp.zeros_like(gk_acc)
        gv_acc[...] = jnp.zeros_like(gv_acc)

        def step(g, carry):
            one_head(kv * GRP + 2 * g)
            one_head(kv * GRP + 2 * g + 1)
            return carry

        lax.fori_loop(0, GRP // 2, step, 0)
        grad_k = gk_acc[...] * scaling
        grad_v = gv_acc[...]
        sa[kv, :, 0] = grad_k[:plen].astype(BF16).reshape(n_r, rows, HD)
        sa[kv, :, 1] = grad_v[:plen].astype(BF16).reshape(n_r, rows, HD)
        for i in range(1, n_r):
            sum_first(kv, row_peer(i), r).start()
        ra[kv, r] = sa[kv, r]
        grk_ref[0, :, lanes] = grad_k[plen:].astype(BF16)
        grv_ref[0, :, lanes] = grad_v[plen:].astype(BF16)
        gq_out(kv).start()

    def gq_out(kv):
        cols = pl.ds(kv * GRP * HD, GRP * HD)
        return pltpu.make_async_copy(gq_v.at[:, cols], gq_hbm.at[0, :, cols], out_sem.at[kv])

    def combine(kv):
        for i in range(1, n_r):
            sum_first(kv, row_peer(i), row_peer(i)).wait_recv()
        sums = [jnp.zeros((2, rows, HD), F32) for _ in range(n_p)]
        for src in range(n_r):
            owner = prompt_of(src)
            term = ra[kv, src].astype(F32)
            for p in range(n_p):
                sums[p] = sums[p] + jnp.where(owner == p, term, 0.0)
        for p in range(n_p):
            sb[kv, p] = sums[p]
        for i in range(1, n_p):
            sum_second(kv, column_peer(i), c).start()

    def finish(kv):
        lanes = slice(kv * HD, (kv + 1) * HD)
        out = sb[kv, c]
        for i in range(1, n_p):
            sum_second(kv, column_peer(i), column_peer(i)).wait_recv()
            out = out + rb[kv, column_peer(i)]
        gpk_ref[0, :, lanes] = out[0]
        gpv_ref[0, :, lanes] = out[1]

    q_in.wait()
    do_in.wait()
    for kv in range(kv_heads):
        attend(kv)
        if kv >= 1:
            combine(kv - 1)
        if kv >= 2:
            finish(kv - 2)
    combine(kv_heads - 1)
    for kv in range(max(kv_heads - 2, 0), kv_heads):
        finish(kv)

    for i in range(1, n_p):
        gather_first(column_peer(i), c).wait_send()
    for kv in range(kv_heads):
        gq_out(kv).wait()
        for i in range(1, n_r):
            gather_second(kv, row_peer(i), r).wait_send()
            sum_first(kv, row_peer(i), r).wait_send()
        for i in range(1, n_p):
            sum_second(kv, column_peer(i), c).wait_send()


def per_device(
    queries,
    resp_keys,
    resp_values,
    grad_out,
    prompt_keys,
    prompt_values,
    group_sizes,
    slot_response,
    lengths,
):
    n_p = lax.axis_size("prompt")
    n_r = lax.axis_size("resp")
    tok = queries.shape[1]
    width = queries.shape[2]
    rows = prompt_keys.shape[1]
    kv_width = prompt_keys.shape[2]
    kv_heads = kv_width // HD
    keys = rows * n_r + tok
    vmem = pl.BlockSpec(memory_space=pltpu.VMEM)
    smem = pl.BlockSpec(memory_space=pltpu.SMEM)
    anywhere = pl.BlockSpec(memory_space=pl.ANY)
    dma = pltpu.SemaphoreType.DMA
    return pl.pallas_call(
        functools.partial(kernel, n_p, n_r),
        out_shape=(
            jax.ShapeDtypeStruct(queries.shape, BF16),
            jax.ShapeDtypeStruct(resp_keys.shape, BF16),
            jax.ShapeDtypeStruct(resp_values.shape, BF16),
            jax.ShapeDtypeStruct(prompt_keys.shape, F32),
            jax.ShapeDtypeStruct(prompt_values.shape, F32),
        ),
        in_specs=[anywhere, anywhere, vmem, vmem, vmem, vmem, smem, smem, smem],
        out_specs=(anywhere, vmem, vmem, vmem, vmem),
        scratch_shapes=[
            pltpu.VMEM((tok, width), BF16),
            pltpu.VMEM((tok, width), BF16),
            pltpu.VMEM((tok, width), BF16),
            pltpu.VMEM((n_p, 2, rows, kv_width), BF16),
            pltpu.VMEM((kv_heads, n_r, 2, rows, HD), BF16),
            pltpu.VMEM((kv_heads, n_r, 2, rows, HD), BF16),
            pltpu.VMEM((kv_heads, n_r, 2, rows, HD), BF16),
            pltpu.VMEM((kv_heads, n_r, 2, rows, HD), BF16),
            pltpu.VMEM((kv_heads, n_p, 2, rows, HD), F32),
            pltpu.VMEM((kv_heads, n_p, 2, rows, HD), F32),
            pltpu.VMEM((keys, HD), BF16),
            pltpu.VMEM((keys, HD), BF16),
            pltpu.VMEM((HD, keys), BF16),
            pltpu.VMEM((keys, HD), F32),
            pltpu.VMEM((keys, HD), F32),
            dma((2,)),
            dma((kv_heads,)),
            dma((n_p,)),
            dma((n_p,)),
            dma((kv_heads, n_r)),
            dma((kv_heads, n_r)),
            dma((kv_heads, n_r)),
            dma((kv_heads, n_r)),
            dma((kv_heads, n_p)),
            dma((kv_heads, n_p)),
        ],
        compiler_params=pltpu.CompilerParams(
            collective_id=0, has_side_effects=True, vmem_limit_bytes=40 * 1024 * 1024
        ),
        cost_estimate=pl.CostEstimate(
            flops=10 * tok * keys * width,
            bytes_accessed=4 * tok * width * 2,
            transcendentals=tok * keys * width // HD,
        ),
    )(
        queries,
        grad_out,
        resp_keys,
        resp_values,
        prompt_keys,
        prompt_values,
        group_sizes,
        slot_response,
        lengths,
    )


def solution(mesh):
    in_specs = (
        P(("prompt", "resp"), None, None),
        P(("prompt", "resp"), None, None),
        P(("prompt", "resp"), None, None),
        P(("prompt", "resp"), None, None),
        P("prompt", "resp", None),
        P("prompt", "resp", None),
        P(),
        P(),
        P(("prompt", "resp")),
    )
    out_specs = (
        P(("prompt", "resp"), None, None),
        P(("prompt", "resp"), None, None),
        P(("prompt", "resp"), None, None),
        P("prompt", "resp", None),
        P("prompt", "resp", None),
    )
    return jax.shard_map(
        per_device, mesh=mesh, in_specs=in_specs, out_specs=out_specs, check_vma=False
    )
```

```python
import functools
import math

import jax
import jax.numpy as jnp
from jax import lax
from jax.experimental import pallas as pl
from jax.experimental.pallas import tpu as pltpu
from jax.sharding import PartitionSpec as P

HD = 128
GRP = 8
VMEM_LIMIT = 60 * 1024 * 1024
MESH = pl.DeviceIdType.MESH
F32 = jnp.float32
BF16 = jnp.bfloat16


def nt(a, b):
    return lax.dot_general(a, b, (((1,), (1,)), ((), ())), preferred_element_type=F32)


def nn(a, b):
    return jnp.dot(a, b, preferred_element_type=F32)


def kernel(
    n_p,
    n_r,
    q_hbm,
    do_hbm,
    rk_hbm,
    rv_hbm,
    pk_hbm,
    pv_hbm,
    sizes_hbm,
    slot_hbm,
    len_hbm,
    gq_out,
    grk_ref,
    grv_ref,
    gpk_ref,
    gpv_ref,
    q_v,
    do_v,
    gq_v,
    sizes_ref,
    slot_ref,
    len_ref,
    g1,
    s2,
    r2,
    sa,
    ra,
    sb,
    rb,
    kall,
    vall,
    ktall,
    gk_acc,
    gv_acc,
    s_0,
    s_1,
    d_0,
    d_1,
    p_0,
    p_1,
    ds_0,
    ds_1,
    m_0,
    m_1,
    in_sem,
    kv_sem,
    out_sem,
    g1_send,
    g1_recv,
    s2_send,
    s2_recv,
    a_send,
    a_recv,
    b_send,
    b_recv,
):
    c = lax.axis_index("prompt")
    r = lax.axis_index("resp")
    rows = g1.shape[2]
    kv_heads = kall.shape[0]
    heads = kv_heads * GRP
    tok = q_v.shape[0]
    plen = rows * n_r
    half = tok // 2
    top = plen + half
    keys = plen + tok
    scaling = 1.0 / math.sqrt(HD)
    to_exp2 = scaling * math.log2(math.e)

    def column_peer(i):
        return lax.rem(c + i, n_p)

    def row_peer(i):
        return lax.rem(r + i, n_r)

    def prompt_of(resp_index):
        value = slot_ref[c * n_r + resp_index]
        end = sizes_ref[0]
        found = (value >= end).astype(jnp.int32)
        for k in range(1, n_p - 1):
            end = end + sizes_ref[k]
            found = found + (value >= end).astype(jnp.int32)
        return found

    first = [
        pltpu.make_async_copy(pk_hbm.at[0], g1.at[c, 0], in_sem.at[0]),
        pltpu.make_async_copy(pv_hbm.at[0], g1.at[c, 1], in_sem.at[1]),
        pltpu.make_async_copy(sizes_hbm, sizes_ref, in_sem.at[2]),
        pltpu.make_async_copy(slot_hbm, slot_ref, in_sem.at[3]),
        pltpu.make_async_copy(len_hbm, len_ref, in_sem.at[4]),
    ]
    q_in = pltpu.make_async_copy(q_hbm.at[0], q_v, in_sem.at[5])
    do_in = pltpu.make_async_copy(do_hbm.at[0], do_v, in_sem.at[6])
    resp_in = []
    for kv in range(kv_heads):
        lanes = pl.ds(kv * HD, HD)
        resp_in.append(
            pltpu.make_async_copy(
                rk_hbm.at[0, :, lanes], kall.at[kv, pl.ds(plen, tok)], kv_sem.at[0, kv]
            )
        )
        resp_in.append(
            pltpu.make_async_copy(
                rv_hbm.at[0, :, lanes], vall.at[kv, pl.ds(plen, tok)], kv_sem.at[1, kv]
            )
        )
    for copy in first + [do_in, q_in] + resp_in:
        copy.start()

    barrier = pltpu.get_barrier_semaphore()
    for i in range(1, n_p):
        pl.semaphore_signal(barrier, inc=1, device_id=(column_peer(i), r), device_id_type=MESH)
    for i in range(1, n_r):
        pl.semaphore_signal(barrier, inc=1, device_id=(c, row_peer(i)), device_id_type=MESH)
    for copy in first:
        copy.wait()
    pl.semaphore_wait(barrier, n_p + n_r - 2)

    def gather_first(to, slot):
        return pltpu.make_async_remote_copy(
            src_ref=g1.at[slot],
            dst_ref=g1.at[slot],
            send_sem=g1_send.at[to],
            recv_sem=g1_recv.at[slot],
            device_id=(to, r),
            device_id_type=MESH,
        )

    def gather_second(kv, to, slot):
        return pltpu.make_async_remote_copy(
            src_ref=s2.at[kv, to],
            dst_ref=r2.at[kv, slot],
            send_sem=s2_send.at[kv, to],
            recv_sem=s2_recv.at[kv, slot],
            device_id=(c, to),
            device_id_type=MESH,
        )

    def sum_first(kv, to, slot):
        return pltpu.make_async_remote_copy(
            src_ref=sa.at[kv, to],
            dst_ref=ra.at[kv, slot],
            send_sem=a_send.at[kv, to],
            recv_sem=a_recv.at[kv, slot],
            device_id=(c, to),
            device_id_type=MESH,
        )

    def sum_second(kv, to, slot):
        return pltpu.make_async_remote_copy(
            src_ref=sb.at[kv, to],
            dst_ref=rb.at[kv, slot],
            send_sem=b_send.at[kv, to],
            recv_sem=b_recv.at[kv, slot],
            device_id=(to, r),
            device_id_type=MESH,
        )

    for i in range(1, n_p):
        gather_first(column_peer(i), c).start()
    gk_acc[...] = jnp.zeros_like(gk_acc)
    gv_acc[...] = jnp.zeros_like(gv_acc)
    for ref in (p_0, p_1, ds_0, ds_1):
        ref[...] = jnp.zeros_like(ref)
    for i in range(1, n_p):
        gather_first(column_peer(i), column_peer(i)).wait_recv()
    for kv in range(kv_heads):
        lanes = slice(kv * HD, (kv + 1) * HD)
        for i in range(1, n_r):
            to = row_peer(i)
            s2[kv, to] = g1[prompt_of(to), :, :, lanes]
            gather_second(kv, to, r).start()
        r2[kv, r] = g1[prompt_of(r), :, :, lanes]

    do_in.wait()
    live_mask = lax.broadcasted_iota(jnp.int32, (tok, HD), 0) < len_ref[0]

    def mask_rows(head, carry):
        lanes = pl.ds(pl.multiple_of(head * HD, HD), HD)
        do_v[:, lanes] = jnp.where(live_mask, do_v[:, lanes], jnp.zeros((), BF16))
        return carry

    lax.fori_loop(0, heads, mask_rows, 0)
    q_in.wait()
    for copy in resp_in:
        copy.wait()

    slots = ((s_0, d_0, p_0, ds_0, m_0), (s_1, d_1, p_1, ds_1, m_1))

    def head_lanes(head):
        return pl.ds(pl.multiple_of(head * HD, HD), HD)

    def load_keys(kv):
        for i in range(1, n_r):
            gather_second(kv, row_peer(i), row_peer(i)).wait_recv()
        kall[kv, :plen] = r2[kv, :, 0].reshape(plen, HD)
        vall[kv, :plen] = r2[kv, :, 1].reshape(plen, HD)
        ktall[kv] = jnp.transpose(kall[kv].astype(F32)).astype(BF16)

    def scores(head, slot):
        s_ref, m_ref = slot[0], slot[4]
        s = nt(kall[head // GRP], q_v[:, head_lanes(head)])
        causal = lax.broadcasted_iota(jnp.int32, (half, half), 0) <= lax.broadcasted_iota(
            jnp.int32, (half, half), 1
        )
        s_p = s[:plen]
        s_l = jnp.where(causal, s[plen:top, :half], -jnp.inf)
        s_r = s[plen:top, half:]
        s_b = jnp.where(causal, s[top:, half:], -jnp.inf)
        s_ref[:plen] = s_p
        s_ref[plen:top, :half] = s_l
        s_ref[plen:top, half:] = s_r
        s_ref[top:, half:] = s_b
        m_p = jnp.max(s_p, axis=0, keepdims=True)
        m_l = jnp.max(s_l, axis=0, keepdims=True)
        m_r = jnp.max(jnp.maximum(s_r, s_b), axis=0, keepdims=True)
        m_ref[...] = jnp.maximum(m_p, jnp.concatenate([m_l, m_r], axis=1)) * to_exp2

    def value_products(head, slot):
        slot[1][...] = nt(vall[head // GRP], do_v[:, head_lanes(head)])

    def add_key_grad(head, slot):
        gk_acc[head // GRP] += nn(slot[3][...], q_v[:, head_lanes(head)])

    def add_value_grad(head, slot):
        gv_acc[head // GRP] += nn(slot[2][...], do_v[:, head_lanes(head)])

    def query_grad(head, slot):
        g_t = nn(ktall[head // GRP], slot[3][...]) * scaling
        gq_v[:, head_lanes(head)] = jnp.transpose(g_t).astype(BF16)

    quarter = half // 2

    def blocks(side):
        limit = top if side == 0 else keys
        return [(low, low + quarter) for low in range(0, limit, quarter)]

    def column(side):
        return slice(side * half, (side + 1) * half)

    def fold(x):
        return jnp.sum(x.reshape(-1, 8, half), axis=0)

    def exponentials(slot, side):
        s_ref, d_ref, m_ref = slot[0], slot[1], slot[4]
        cols = column(side)
        m = m_ref[:, cols]
        norm = jnp.zeros((8, half), F32)
        dots = jnp.zeros((8, half), F32)
        for low, high in blocks(side):
            e = jnp.exp2(s_ref[low:high, cols] * to_exp2 - m)
            s_ref[low:high, cols] = e
            norm = norm + fold(e)
            dots = dots + fold(e * d_ref[low:high, cols])
        inv = 1.0 / jnp.sum(norm, axis=0, keepdims=True)
        return inv, jnp.sum(dots, axis=0, keepdims=True) * inv

    def differences(slot, side, inv, dot_row):
        s_ref, d_ref, p_ref, ds_ref = slot[:4]
        cols = column(side)
        for low, high in blocks(side):
            p = s_ref[low:high, cols] * inv
            p_ref[low:high, cols] = p.astype(BF16)
            ds_ref[low:high, cols] = (p * (d_ref[low:high, cols] - dot_row)).astype(BF16)

    def step(head, cur, other):
        ahead = jnp.minimum(head + 1, heads - 1)
        behind = jnp.maximum(head - 1, 0)
        scores(ahead, other)
        stats_0 = exponentials(cur, 0)
        add_key_grad(behind, other)
        stats_1 = exponentials(cur, 1)
        add_value_grad(behind, other)
        differences(cur, 0, *stats_0)
        query_grad(behind, other)
        differences(cur, 1, *stats_1)
        value_products(ahead, other)

    def send_sums(kv):
        grad_k = gk_acc[kv] * scaling
        grad_v = gv_acc[kv]
        sa[kv, :, 0] = grad_k[:plen].astype(BF16).reshape(n_r, rows, HD)
        sa[kv, :, 1] = grad_v[:plen].astype(BF16).reshape(n_r, rows, HD)
        for i in range(1, n_r):
            sum_first(kv, row_peer(i), r).start()
        ra[kv, r] = sa[kv, r]
        lanes = head_lanes(kv)
        grk_ref[0, :, lanes] = grad_k[plen:].astype(BF16)
        grv_ref[0, :, lanes] = grad_v[plen:].astype(BF16)
        store_queries(kv).start()

    def store_queries(kv):
        cols = pl.ds(pl.multiple_of(kv * GRP * HD, HD), GRP * HD)
        return pltpu.make_async_copy(gq_v.at[:, cols], gq_out.at[0, :, cols], out_sem.at[kv])

    def combine(kv):
        for i in range(1, n_r):
            sum_first(kv, row_peer(i), row_peer(i)).wait_recv()
        sums = [jnp.zeros((2, rows, HD), F32) for _ in range(n_p)]
        for src in range(n_r):
            owner = prompt_of(src)
            term = ra[kv, src].astype(F32)
            for p in range(n_p):
                sums[p] = sums[p] + jnp.where(owner == p, term, 0.0)
        for p in range(n_p):
            sb[kv, p] = sums[p]
        for i in range(1, n_p):
            sum_second(kv, column_peer(i), c).start()

    def finish(kv):
        lanes = head_lanes(kv)
        out = sb[kv, c]
        for i in range(1, n_p):
            sum_second(kv, column_peer(i), column_peer(i)).wait_recv()
            out = out + rb[kv, column_peer(i)]
        gpk_ref[0, :, lanes] = out[0]
        gpv_ref[0, :, lanes] = out[1]

    load_keys(0)
    scores(0, slots[0])
    value_products(0, slots[0])
    pairs = GRP // 2

    def pair(index, carry):
        kv = index // pairs
        place = index % pairs

        @pl.when((place == pairs - 1) & (kv < kv_heads - 1))
        def _():
            load_keys(kv + 1)

        @pl.when((place == 1) & (kv > 0))
        def _():
            send_sums(kv - 1)

        @pl.when((place == pairs - 1) & (kv > 0))
        def _():
            combine(kv - 1)

        step(2 * index, slots[0], slots[1])
        step(2 * index + 1, slots[1], slots[0])
        return carry

    lax.fori_loop(0, heads // 2, pair, 0)
    add_key_grad(heads - 1, slots[1])
    add_value_grad(heads - 1, slots[1])
    query_grad(heads - 1, slots[1])
    send_sums(kv_heads - 1)
    for kv in range(kv_heads - 1):
        finish(kv)
    combine(kv_heads - 1)
    finish(kv_heads - 1)

    for i in range(1, n_p):
        gather_first(column_peer(i), c).wait_send()
    for kv in range(kv_heads):
        store_queries(kv).wait()
        for i in range(1, n_r):
            gather_second(kv, row_peer(i), r).wait_send()
            sum_first(kv, row_peer(i), r).wait_send()
        for i in range(1, n_p):
            sum_second(kv, column_peer(i), c).wait_send()


def store_kernel(*refs):
    count = (len(refs) - 1) // 2
    sem = refs[-1]
    copies = [
        pltpu.make_async_copy(refs[k], refs[count + k], sem.at[k]) for k in range(count)
    ]
    for copy in copies:
        copy.start()
    for copy in copies:
        copy.wait()


def per_device(
    queries,
    resp_keys,
    resp_values,
    grad_out,
    prompt_keys,
    prompt_values,
    group_sizes,
    slot_response,
    lengths,
):
    n_p = lax.axis_size("prompt")
    n_r = lax.axis_size("resp")
    tok = queries.shape[1]
    width = queries.shape[2]
    rows = prompt_keys.shape[1]
    kv_width = prompt_keys.shape[2]
    kv_heads = kv_width // HD
    keys = rows * n_r + tok
    vmem = pl.BlockSpec(memory_space=pltpu.VMEM)
    hbm = pl.BlockSpec(memory_space=pltpu.HBM)
    anywhere = pl.BlockSpec(memory_space=pl.ANY)
    dma = pltpu.SemaphoreType.DMA
    out_shape = (
        jax.ShapeDtypeStruct(queries.shape, BF16),
        jax.ShapeDtypeStruct(resp_keys.shape, BF16),
        jax.ShapeDtypeStruct(resp_values.shape, BF16),
        jax.ShapeDtypeStruct(prompt_keys.shape, F32),
        jax.ShapeDtypeStruct(prompt_values.shape, F32),
    )
    results = pl.pallas_call(
        functools.partial(kernel, n_p, n_r),
        out_shape=out_shape,
        in_specs=[hbm] * 9,
        out_specs=(anywhere, vmem, vmem, vmem, vmem),
        scratch_shapes=[
            pltpu.VMEM((tok, width), BF16),
            pltpu.VMEM((tok, width), BF16),
            pltpu.VMEM((tok, width), BF16),
            pltpu.SMEM(group_sizes.shape, jnp.int32),
            pltpu.SMEM(slot_response.shape, jnp.int32),
            pltpu.SMEM(lengths.shape, jnp.int32),
            pltpu.VMEM((n_p, 2, rows, kv_width), BF16),
            pltpu.VMEM((kv_heads, n_r, 2, rows, HD), BF16),
            pltpu.VMEM((kv_heads, n_r, 2, rows, HD), BF16),
            pltpu.VMEM((kv_heads, n_r, 2, rows, HD), BF16),
            pltpu.VMEM((kv_heads, n_r, 2, rows, HD), BF16),
            pltpu.VMEM((kv_heads, n_p, 2, rows, HD), F32),
            pltpu.VMEM((kv_heads, n_p, 2, rows, HD), F32),
            pltpu.VMEM((kv_heads, keys, HD), BF16),
            pltpu.VMEM((kv_heads, keys, HD), BF16),
            pltpu.VMEM((kv_heads, HD, keys), BF16),
            pltpu.VMEM((kv_heads, keys, HD), F32),
            pltpu.VMEM((kv_heads, keys, HD), F32),
            pltpu.VMEM((keys, tok), F32),
            pltpu.VMEM((keys, tok), F32),
            pltpu.VMEM((keys, tok), F32),
            pltpu.VMEM((keys, tok), F32),
            pltpu.VMEM((keys, tok), BF16),
            pltpu.VMEM((keys, tok), BF16),
            pltpu.VMEM((keys, tok), BF16),
            pltpu.VMEM((keys, tok), BF16),
            pltpu.VMEM((1, tok), F32),
            pltpu.VMEM((1, tok), F32),
            dma((7,)),
            dma((2, kv_heads)),
            dma((kv_heads,)),
            dma((n_p,)),
            dma((n_p,)),
            dma((kv_heads, n_r)),
            dma((kv_heads, n_r)),
            dma((kv_heads, n_r)),
            dma((kv_heads, n_r)),
            dma((kv_heads, n_p)),
            dma((kv_heads, n_p)),
        ],
        compiler_params=pltpu.CompilerParams(
            collective_id=0, has_side_effects=True, vmem_limit_bytes=VMEM_LIMIT
        ),
        cost_estimate=pl.CostEstimate(
            flops=10 * tok * keys * width,
            bytes_accessed=4 * tok * width * 2,
            transcendentals=tok * keys * width // HD,
        ),
    )(
        queries,
        grad_out,
        resp_keys,
        resp_values,
        prompt_keys,
        prompt_values,
        group_sizes,
        slot_response,
        lengths,
    )
    return pl.pallas_call(
        store_kernel,
        out_shape=out_shape,
        in_specs=[anywhere] * len(out_shape),
        out_specs=(hbm,) * len(out_shape),
        scratch_shapes=[dma((len(out_shape),))],
        compiler_params=pltpu.CompilerParams(vmem_limit_bytes=VMEM_LIMIT),
    )(*results)


def solution(mesh):
    in_specs = (
        P(("prompt", "resp"), None, None),
        P(("prompt", "resp"), None, None),
        P(("prompt", "resp"), None, None),
        P(("prompt", "resp"), None, None),
        P("prompt", "resp", None),
        P("prompt", "resp", None),
        P(),
        P(),
        P(("prompt", "resp")),
    )
    out_specs = (
        P(("prompt", "resp"), None, None),
        P(("prompt", "resp"), None, None),
        P(("prompt", "resp"), None, None),
        P("prompt", "resp", None),
        P("prompt", "resp", None),
    )
    return jax.shard_map(
        per_device, mesh=mesh, in_specs=in_specs, out_specs=out_specs, check_vma=False
    )
```

```python
import functools
import math

import jax
import jax.numpy as jnp
from jax import lax
from jax.experimental import pallas as pl
from jax.experimental.pallas import tpu as pltpu
from jax.sharding import PartitionSpec as P

HD = 128
GRP = 8
VMEM_LIMIT = 60 * 1024 * 1024
MESH = pl.DeviceIdType.MESH
F32 = jnp.float32
BF16 = jnp.bfloat16


def nt(a, b):
    return lax.dot_general(a, b, (((1,), (1,)), ((), ())), preferred_element_type=F32)


def nn(a, b):
    return jnp.dot(a, b, preferred_element_type=F32)


def places(n_p, n_r):
    c = lax.axis_index("prompt")
    r = lax.axis_index("resp")
    columns = [lax.rem(c + i, n_p) for i in range(1, n_p)]
    partners = [lax.rem(r + i, n_r) for i in range(1, n_r)]
    return c, r, columns, partners


def prompt_of(sizes_ref, slot_ref, n_p, index):
    value = slot_ref[index]
    end = sizes_ref[0]
    found = (value >= end).astype(jnp.int32)
    for k in range(1, n_p - 1):
        end = end + sizes_ref[k]
        found = found + (value >= end).astype(jnp.int32)
    return found


def greet(c, r, columns, partners):
    barrier = pltpu.get_barrier_semaphore()
    for to in columns:
        pl.semaphore_signal(barrier, inc=1, device_id=(to, r), device_id_type=MESH)
    for to in partners:
        pl.semaphore_signal(barrier, inc=1, device_id=(c, to), device_id_type=MESH)
    pl.semaphore_wait(barrier, len(columns) + len(partners))


def send(src, dst, send_sem, recv_sem, device):
    return pltpu.make_async_remote_copy(
        src_ref=src,
        dst_ref=dst,
        send_sem=send_sem,
        recv_sem=recv_sem,
        device_id=device,
        device_id_type=MESH,
    )


def gather_kernel(
    n_p, n_r, pk_ref, pv_ref, sizes_ref, slot_ref, out_ref, g1, s2, r2, s_1, r_1, s_2, r_2
):
    c, r, columns, partners = places(n_p, n_r)
    g1[c, 0] = pk_ref[0]
    g1[c, 1] = pv_ref[0]
    greet(c, r, columns, partners)

    def first(to, slot):
        return send(g1.at[slot], g1.at[slot], s_1.at[to], r_1.at[slot], (to, r))

    def second(to, slot):
        return send(s2.at[to], r2.at[slot], s_2.at[to], r_2.at[slot], (c, to))

    for to in columns:
        first(to, c).start()
    for to in columns:
        first(to, to).wait_recv()
    for to in partners:
        s2[to] = g1[prompt_of(sizes_ref, slot_ref, n_p, c * n_r + to)]
        second(to, r).start()
    r2[r] = g1[prompt_of(sizes_ref, slot_ref, n_p, c * n_r + r)]
    for to in partners:
        second(to, to).wait_recv()
    out_ref[...] = r2[...]
    for to in columns:
        first(to, c).wait_send()
    for to in partners:
        second(to, r).wait_send()


def sum_kernel(
    n_p, n_r, sa, sizes_ref, slot_ref, gpk_ref, gpv_ref, ra, sb, rb, s_1, r_1, s_2, r_2
):
    c, r, columns, partners = places(n_p, n_r)
    rows = gpk_ref.shape[1]
    width = gpk_ref.shape[2]
    greet(c, r, columns, partners)

    def first(to, slot):
        return send(sa.at[to], ra.at[slot], s_1.at[to], r_1.at[slot], (c, to))

    def second(to, slot):
        return send(sb.at[to], rb.at[slot], s_2.at[to], r_2.at[slot], (to, r))

    for to in partners:
        first(to, r).start()
    ra[r] = sa[r]
    for to in partners:
        first(to, to).wait_recv()
    owners = [prompt_of(sizes_ref, slot_ref, n_p, c * n_r + src) for src in range(n_r)]
    for low in range(0, width, HD):
        lanes = slice(low, low + HD)
        sums = [jnp.zeros((2, rows, HD), F32) for _ in range(n_p)]
        for src in range(n_r):
            term = ra[src, :, :, lanes].astype(F32)
            for p in range(n_p):
                sums[p] = sums[p] + jnp.where(owners[src] == p, term, 0.0)
        for p in range(n_p):
            sb[p, :, :, lanes] = sums[p]
    for to in columns:
        second(to, c).start()
    out = sb[c]
    for to in columns:
        second(to, to).wait_recv()
        out = out + rb[to]
    gpk_ref[0] = out[0]
    gpv_ref[0] = out[1]
    for to in partners:
        first(to, r).wait_send()
    for to in columns:
        second(to, c).wait_send()


def attend_kernel(
    q_hbm,
    do_hbm,
    rk_ref,
    rv_ref,
    own_ref,
    len_ref,
    gq_out,
    grk_ref,
    grv_ref,
    sums_ref,
    q_v,
    do_v,
    gq_v,
    kall,
    vall,
    ktall,
    gk_acc,
    gv_acc,
    s_0,
    s_1,
    d_0,
    d_1,
    p_0,
    p_1,
    ds_0,
    ds_1,
    m_0,
    m_1,
    in_sem,
    out_sem,
):
    n_r, _, rows, _ = own_ref.shape
    kv_heads = kall.shape[0]
    heads = kv_heads * GRP
    tok = q_v.shape[0]
    plen = rows * n_r
    half = tok // 2
    top = plen + half
    keys = plen + tok
    scaling = 1.0 / math.sqrt(HD)
    to_exp2 = scaling * math.log2(math.e)

    def group_lanes(kv):
        return pl.ds(pl.multiple_of(kv * GRP * HD, HD), GRP * HD)

    def queries_in(kv):
        lanes = group_lanes(kv)
        return pltpu.make_async_copy(q_hbm.at[0, :, lanes], q_v.at[:, lanes], in_sem.at[0, kv])

    def upstream_in(kv):
        lanes = group_lanes(kv)
        return pltpu.make_async_copy(do_hbm.at[0, :, lanes], do_v.at[:, lanes], in_sem.at[1, kv])

    for kv in range(kv_heads):
        queries_in(kv).start()
        upstream_in(kv).start()
    gk_acc[...] = jnp.zeros_like(gk_acc)
    gv_acc[...] = jnp.zeros_like(gv_acc)
    for ref in (p_0, p_1, ds_0, ds_1):
        ref[...] = jnp.zeros_like(ref)
    live_mask = lax.broadcasted_iota(jnp.int32, (tok, HD), 0) < len_ref[0]
    slots = ((s_0, d_0, p_0, ds_0, m_0), (s_1, d_1, p_1, ds_1, m_1))

    def head_lanes(head):
        return pl.ds(pl.multiple_of(head * HD, HD), HD)

    def load_group(kv):
        lanes = head_lanes(kv)
        kall[kv, :plen] = own_ref[:, 0, :, lanes].reshape(plen, HD)
        vall[kv, :plen] = own_ref[:, 1, :, lanes].reshape(plen, HD)
        kall[kv, plen:] = rk_ref[0, :, lanes]
        vall[kv, plen:] = rv_ref[0, :, lanes]
        ktall[kv] = jnp.transpose(kall[kv].astype(F32)).astype(BF16)
        queries_in(kv).wait()
        upstream_in(kv).wait()

        def mask_rows(i, carry):
            cols = head_lanes(kv * GRP + i)
            do_v[:, cols] = jnp.where(live_mask, do_v[:, cols], jnp.zeros((), BF16))
            return carry

        lax.fori_loop(0, GRP, mask_rows, 0)

    def scores(head, slot):
        s_ref, m_ref = slot[0], slot[4]
        s = nt(kall[head // GRP], q_v[:, head_lanes(head)])
        causal = lax.broadcasted_iota(jnp.int32, (half, half), 0) <= lax.broadcasted_iota(
            jnp.int32, (half, half), 1
        )
        s_p = s[:plen]
        s_l = jnp.where(causal, s[plen:top, :half], -jnp.inf)
        s_r = s[plen:top, half:]
        s_b = jnp.where(causal, s[top:, half:], -jnp.inf)
        s_ref[:plen] = s_p
        s_ref[plen:top, :half] = s_l
        s_ref[plen:top, half:] = s_r
        s_ref[top:, half:] = s_b
        m_p = jnp.max(s_p, axis=0, keepdims=True)
        m_l = jnp.max(s_l, axis=0, keepdims=True)
        m_r = jnp.max(jnp.maximum(s_r, s_b), axis=0, keepdims=True)
        m_ref[...] = jnp.maximum(m_p, jnp.concatenate([m_l, m_r], axis=1)) * to_exp2

    def value_products(head, slot):
        slot[1][...] = nt(vall[head // GRP], do_v[:, head_lanes(head)])

    def add_key_grad(head, slot):
        gk_acc[head // GRP] += nn(slot[3][...], q_v[:, head_lanes(head)])

    def add_value_grad(head, slot):
        gv_acc[head // GRP] += nn(slot[2][...], do_v[:, head_lanes(head)])

    def query_grad(head, slot):
        g_t = nn(ktall[head // GRP], slot[3][...]) * scaling
        gq_v[:, head_lanes(head)] = jnp.transpose(g_t).astype(BF16)

    quarter = half // 2

    def blocks(side):
        limit = top if side == 0 else keys
        return [(low, low + quarter) for low in range(0, limit, quarter)]

    def column(side):
        return slice(side * half, (side + 1) * half)

    def fold(x):
        return jnp.sum(x.reshape(-1, 8, half), axis=0)

    def exponentials(slot, side):
        s_ref, d_ref, m_ref = slot[0], slot[1], slot[4]
        cols = column(side)
        m = m_ref[:, cols]
        norm = jnp.zeros((8, half), F32)
        dots = jnp.zeros((8, half), F32)
        for low, high in blocks(side):
            e = jnp.exp2(s_ref[low:high, cols] * to_exp2 - m)
            s_ref[low:high, cols] = e
            norm = norm + fold(e)
            dots = dots + fold(e * d_ref[low:high, cols])
        inv = 1.0 / jnp.sum(norm, axis=0, keepdims=True)
        return inv, jnp.sum(dots, axis=0, keepdims=True) * inv

    def differences(slot, side, inv, dot_row):
        s_ref, d_ref, p_ref, ds_ref = slot[:4]
        cols = column(side)
        for low, high in blocks(side):
            p = s_ref[low:high, cols] * inv
            p_ref[low:high, cols] = p.astype(BF16)
            ds_ref[low:high, cols] = (p * (d_ref[low:high, cols] - dot_row)).astype(BF16)

    def step(head, cur, other):
        ahead = jnp.minimum(head + 1, heads - 1)
        behind = jnp.maximum(head - 1, 0)
        scores(ahead, other)
        stats_0 = exponentials(cur, 0)
        add_key_grad(behind, other)
        stats_1 = exponentials(cur, 1)
        add_value_grad(behind, other)
        differences(cur, 0, *stats_0)
        query_grad(behind, other)
        differences(cur, 1, *stats_1)
        value_products(ahead, other)

    def store_queries(kv):
        lanes = group_lanes(kv)
        return pltpu.make_async_copy(gq_v.at[:, lanes], gq_out.at[0, :, lanes], out_sem.at[kv])

    def store_group(kv):
        lanes = head_lanes(kv)
        grad_k = gk_acc[kv] * scaling
        grad_v = gv_acc[kv]
        sums_ref[:, 0, :, lanes] = grad_k[:plen].astype(BF16).reshape(n_r, rows, HD)
        sums_ref[:, 1, :, lanes] = grad_v[:plen].astype(BF16).reshape(n_r, rows, HD)
        grk_ref[0, :, lanes] = grad_k[plen:].astype(BF16)
        grv_ref[0, :, lanes] = grad_v[plen:].astype(BF16)
        store_queries(kv).start()

    load_group(0)
    scores(0, slots[0])
    value_products(0, slots[0])
    pairs = GRP // 2

    def pair(index, carry):
        kv = index // pairs
        place = index % pairs

        @pl.when((place == pairs - 1) & (kv < kv_heads - 1))
        def _():
            load_group(kv + 1)

        @pl.when((place == 1) & (kv > 0))
        def _():
            store_group(kv - 1)

        step(2 * index, slots[0], slots[1])
        step(2 * index + 1, slots[1], slots[0])
        return carry

    lax.fori_loop(0, heads // 2, pair, 0)
    add_key_grad(heads - 1, slots[1])
    add_value_grad(heads - 1, slots[1])
    query_grad(heads - 1, slots[1])
    store_group(kv_heads - 1)
    for kv in range(kv_heads):
        store_queries(kv).wait()


def per_device(
    queries,
    resp_keys,
    resp_values,
    grad_out,
    prompt_keys,
    prompt_values,
    group_sizes,
    slot_response,
    lengths,
):
    n_p = lax.axis_size("prompt")
    n_r = lax.axis_size("resp")
    tok = queries.shape[1]
    width = queries.shape[2]
    rows = prompt_keys.shape[1]
    kv_width = prompt_keys.shape[2]
    kv_heads = kv_width // HD
    keys = rows * n_r + tok
    vmem = pl.BlockSpec(memory_space=pltpu.VMEM)
    smem = pl.BlockSpec(memory_space=pltpu.SMEM)
    hbm = pl.BlockSpec(memory_space=pltpu.HBM)
    dma = pltpu.SemaphoreType.DMA
    own = pl.pallas_call(
        functools.partial(gather_kernel, n_p, n_r),
        out_shape=jax.ShapeDtypeStruct((n_r, 2, rows, kv_width), BF16),
        in_specs=[vmem, vmem, smem, smem],
        out_specs=vmem,
        scratch_shapes=[
            pltpu.VMEM((n_p, 2, rows, kv_width), BF16),
            pltpu.VMEM((n_r, 2, rows, kv_width), BF16),
            pltpu.VMEM((n_r, 2, rows, kv_width), BF16),
            dma((n_p,)),
            dma((n_p,)),
            dma((n_r,)),
            dma((n_r,)),
        ],
        compiler_params=pltpu.CompilerParams(
            collective_id=0, has_side_effects=True, vmem_limit_bytes=VMEM_LIMIT
        ),
    )(prompt_keys, prompt_values, group_sizes, slot_response)
    grad_q, grad_rk, grad_rv, sums = pl.pallas_call(
        attend_kernel,
        out_shape=(
            jax.ShapeDtypeStruct(queries.shape, BF16),
            jax.ShapeDtypeStruct(resp_keys.shape, BF16),
            jax.ShapeDtypeStruct(resp_values.shape, BF16),
            jax.ShapeDtypeStruct((n_r, 2, rows, kv_width), BF16),
        ),
        in_specs=[hbm, hbm, vmem, vmem, vmem, smem],
        out_specs=(hbm, vmem, vmem, vmem),
        scratch_shapes=[
            pltpu.VMEM((tok, width), BF16),
            pltpu.VMEM((tok, width), BF16),
            pltpu.VMEM((tok, width), BF16),
            pltpu.VMEM((kv_heads, keys, HD), BF16),
            pltpu.VMEM((kv_heads, keys, HD), BF16),
            pltpu.VMEM((kv_heads, HD, keys), BF16),
            pltpu.VMEM((kv_heads, keys, HD), F32),
            pltpu.VMEM((kv_heads, keys, HD), F32),
            pltpu.VMEM((keys, tok), F32),
            pltpu.VMEM((keys, tok), F32),
            pltpu.VMEM((keys, tok), F32),
            pltpu.VMEM((keys, tok), F32),
            pltpu.VMEM((keys, tok), BF16),
            pltpu.VMEM((keys, tok), BF16),
            pltpu.VMEM((keys, tok), BF16),
            pltpu.VMEM((keys, tok), BF16),
            pltpu.VMEM((1, tok), F32),
            pltpu.VMEM((1, tok), F32),
            dma((2, kv_heads)),
            dma((kv_heads,)),
        ],
        compiler_params=pltpu.CompilerParams(vmem_limit_bytes=VMEM_LIMIT),
    )(queries, grad_out, resp_keys, resp_values, own, lengths)
    grad_pk, grad_pv = pl.pallas_call(
        functools.partial(sum_kernel, n_p, n_r),
        out_shape=(
            jax.ShapeDtypeStruct(prompt_keys.shape, F32),
            jax.ShapeDtypeStruct(prompt_values.shape, F32),
        ),
        in_specs=[vmem, smem, smem],
        out_specs=(vmem, vmem),
        scratch_shapes=[
            pltpu.VMEM((n_r, 2, rows, kv_width), BF16),
            pltpu.VMEM((n_p, 2, rows, kv_width), F32),
            pltpu.VMEM((n_p, 2, rows, kv_width), F32),
            dma((n_r,)),
            dma((n_r,)),
            dma((n_p,)),
            dma((n_p,)),
        ],
        compiler_params=pltpu.CompilerParams(
            collective_id=1, has_side_effects=True, vmem_limit_bytes=VMEM_LIMIT
        ),
    )(sums, group_sizes, slot_response)
    return grad_q, grad_rk, grad_rv, grad_pk, grad_pv


def solution(mesh):
    in_specs = (
        P(("prompt", "resp"), None, None),
        P(("prompt", "resp"), None, None),
        P(("prompt", "resp"), None, None),
        P(("prompt", "resp"), None, None),
        P("prompt", "resp", None),
        P("prompt", "resp", None),
        P(),
        P(),
        P(("prompt", "resp")),
    )
    out_specs = (
        P(("prompt", "resp"), None, None),
        P(("prompt", "resp"), None, None),
        P(("prompt", "resp"), None, None),
        P("prompt", "resp", None),
        P("prompt", "resp", None),
    )
    return jax.shard_map(
        per_device, mesh=mesh, in_specs=in_specs, out_specs=out_specs, check_vma=False
    )
```

```python
import functools
import math

import jax
import jax.numpy as jnp
from jax import lax
from jax.experimental import pallas as pl
from jax.experimental.pallas import tpu as pltpu
from jax.sharding import PartitionSpec as P

HD = 128
GRP = 8
VMEM_LIMIT = 60 * 1024 * 1024
MESH = pl.DeviceIdType.MESH
F32 = jnp.float32
BF16 = jnp.bfloat16


def nt(a, b):
    return lax.dot_general(a, b, (((1,), (1,)), ((), ())), preferred_element_type=F32)


def nn(a, b):
    return jnp.dot(a, b, preferred_element_type=F32)


def kernel(
    n_p,
    n_r,
    q_hbm,
    do_hbm,
    rk_hbm,
    rv_hbm,
    pk_hbm,
    pv_hbm,
    sizes_hbm,
    slot_hbm,
    len_hbm,
    gq_out,
    grk_ref,
    grv_ref,
    gpk_ref,
    gpv_ref,
    q_v,
    do_v,
    gq_v,
    sizes_ref,
    slot_ref,
    len_ref,
    own,
    g1,
    s2,
    r2,
    sa,
    ra,
    sb,
    rb,
    kall,
    vall,
    ktall,
    gk_acc,
    gv_acc,
    s_0,
    s_1,
    d_0,
    d_1,
    p_0,
    p_1,
    ds_0,
    ds_1,
    m_0,
    m_1,
    in_sem,
    kv_sem,
    out_sem,
    g1_send,
    g1_recv,
    s2_send,
    s2_recv,
    a_send,
    a_recv,
    b_send,
    b_recv,
):
    c = lax.axis_index("prompt")
    r = lax.axis_index("resp")
    rows = g1.shape[3]
    kv_heads = kall.shape[0]
    heads = kv_heads * GRP
    tok = q_v.shape[0]
    plen = rows * n_r
    half = tok // 2
    top = plen + half
    keys = plen + tok
    scaling = 1.0 / math.sqrt(HD)
    to_exp2 = scaling * math.log2(math.e)

    def column_peer(i):
        return lax.rem(c + i, n_p)

    def row_peer(i):
        return lax.rem(r + i, n_r)

    def prompt_of(resp_index):
        value = slot_ref[c * n_r + resp_index]
        end = sizes_ref[0]
        found = (value >= end).astype(jnp.int32)
        for k in range(1, n_p - 1):
            end = end + sizes_ref[k]
            found = found + (value >= end).astype(jnp.int32)
        return found

    first = [
        pltpu.make_async_copy(pk_hbm.at[0], own.at[0], in_sem.at[0]),
        pltpu.make_async_copy(pv_hbm.at[0], own.at[1], in_sem.at[1]),
        pltpu.make_async_copy(sizes_hbm, sizes_ref, in_sem.at[2]),
        pltpu.make_async_copy(slot_hbm, slot_ref, in_sem.at[3]),
        pltpu.make_async_copy(len_hbm, len_ref, in_sem.at[4]),
    ]
    q_in = pltpu.make_async_copy(q_hbm.at[0], q_v, in_sem.at[5])
    do_in = pltpu.make_async_copy(do_hbm.at[0], do_v, in_sem.at[6])
    resp_in = []
    for kv in range(kv_heads):
        lanes = pl.ds(kv * HD, HD)
        resp_in.append(
            pltpu.make_async_copy(
                rk_hbm.at[0, :, lanes], kall.at[kv, pl.ds(plen, tok)], kv_sem.at[0, kv]
            )
        )
        resp_in.append(
            pltpu.make_async_copy(
                rv_hbm.at[0, :, lanes], vall.at[kv, pl.ds(plen, tok)], kv_sem.at[1, kv]
            )
        )
    for copy in first + [do_in, q_in] + resp_in:
        copy.start()

    barrier = pltpu.get_barrier_semaphore()
    for i in range(1, n_p):
        pl.semaphore_signal(barrier, inc=1, device_id=(column_peer(i), r), device_id_type=MESH)
    for i in range(1, n_r):
        pl.semaphore_signal(barrier, inc=1, device_id=(c, row_peer(i)), device_id_type=MESH)
    for copy in first:
        copy.wait()
    for kv in range(kv_heads):
        g1[kv, c] = own[:, :, kv * HD : (kv + 1) * HD]
    pl.semaphore_wait(barrier, n_p + n_r - 2)

    def gather_first(kv, to, slot):
        return pltpu.make_async_remote_copy(
            src_ref=g1.at[kv, slot],
            dst_ref=g1.at[kv, slot],
            send_sem=g1_send.at[kv, to],
            recv_sem=g1_recv.at[kv, slot],
            device_id=(to, r),
            device_id_type=MESH,
        )

    def gather_second(kv, to, slot):
        return pltpu.make_async_remote_copy(
            src_ref=s2.at[kv, to],
            dst_ref=r2.at[kv, slot],
            send_sem=s2_send.at[kv, to],
            recv_sem=s2_recv.at[kv, slot],
            device_id=(c, to),
            device_id_type=MESH,
        )

    def sum_first(kv, to, slot):
        return pltpu.make_async_remote_copy(
            src_ref=sa.at[kv, to],
            dst_ref=ra.at[kv, slot],
            send_sem=a_send.at[kv, to],
            recv_sem=a_recv.at[kv, slot],
            device_id=(c, to),
            device_id_type=MESH,
        )

    def sum_second(kv, to, slot):
        return pltpu.make_async_remote_copy(
            src_ref=sb.at[kv, to],
            dst_ref=rb.at[kv, slot],
            send_sem=b_send.at[kv, to],
            recv_sem=b_recv.at[kv, slot],
            device_id=(to, r),
            device_id_type=MESH,
        )

    def send_first(kv):
        for i in range(1, n_p):
            gather_first(kv, column_peer(i), c).start()

    def picked(kv, to):
        owner = prompt_of(to)
        block = g1[kv, 0]
        for p in range(1, n_p):
            block = jnp.where(owner == p, g1[kv, p], block)
        return block

    def send_second(kv):
        for i in range(1, n_p):
            gather_first(kv, column_peer(i), column_peer(i)).wait_recv()
        for i in range(1, n_r):
            to = row_peer(i)
            s2[kv, to] = picked(kv, to)
            gather_second(kv, to, r).start()
        r2[kv, r] = picked(kv, r)

    send_first(0)
    send_second(0)
    for kv in range(1, kv_heads):
        send_first(kv)
    gk_acc[...] = jnp.zeros_like(gk_acc)
    gv_acc[...] = jnp.zeros_like(gv_acc)
    for ref in (p_0, p_1, ds_0, ds_1):
        ref[...] = jnp.zeros_like(ref)
    do_in.wait()
    live_mask = lax.broadcasted_iota(jnp.int32, (tok, HD), 0) < len_ref[0]

    def mask_rows(head, carry):
        lanes = pl.ds(pl.multiple_of(head * HD, HD), HD)
        do_v[:, lanes] = jnp.where(live_mask, do_v[:, lanes], jnp.zeros((), BF16))
        return carry

    lax.fori_loop(0, heads, mask_rows, 0)
    q_in.wait()
    for copy in resp_in:
        copy.wait()

    slots = ((s_0, d_0, p_0, ds_0, m_0), (s_1, d_1, p_1, ds_1, m_1))

    def head_lanes(head):
        return pl.ds(pl.multiple_of(head * HD, HD), HD)

    def load_keys(kv):
        for i in range(1, n_r):
            gather_second(kv, row_peer(i), row_peer(i)).wait_recv()

        @pl.when(kv < kv_heads - 1)
        def _():
            send_second(kv + 1)

        kall[kv, :plen] = r2[kv, :, 0].reshape(plen, HD)
        vall[kv, :plen] = r2[kv, :, 1].reshape(plen, HD)
        ktall[kv] = jnp.transpose(kall[kv].astype(F32)).astype(BF16)

    def scores(head, slot):
        s_ref, m_ref = slot[0], slot[4]
        s = nt(kall[head // GRP], q_v[:, head_lanes(head)])
        causal = lax.broadcasted_iota(jnp.int32, (half, half), 0) <= lax.broadcasted_iota(
            jnp.int32, (half, half), 1
        )
        s_p = s[:plen]
        s_l = jnp.where(causal, s[plen:top, :half], -jnp.inf)
        s_r = s[plen:top, half:]
        s_b = jnp.where(causal, s[top:, half:], -jnp.inf)
        s_ref[:plen] = s_p
        s_ref[plen:top, :half] = s_l
        s_ref[plen:top, half:] = s_r
        s_ref[top:, half:] = s_b
        m_p = jnp.max(s_p, axis=0, keepdims=True)
        m_l = jnp.max(s_l, axis=0, keepdims=True)
        m_r = jnp.max(jnp.maximum(s_r, s_b), axis=0, keepdims=True)
        m_ref[...] = jnp.maximum(m_p, jnp.concatenate([m_l, m_r], axis=1)) * to_exp2

    def value_products(head, slot):
        slot[1][...] = nt(vall[head // GRP], do_v[:, head_lanes(head)])

    def add_key_grad(head, slot):
        gk_acc[head // GRP] += nn(slot[3][...], q_v[:, head_lanes(head)])

    def add_value_grad(head, slot):
        gv_acc[head // GRP] += nn(slot[2][...], do_v[:, head_lanes(head)])

    def query_grad(head, slot):
        g_t = nn(ktall[head // GRP], slot[3][...]) * scaling
        gq_v[:, head_lanes(head)] = jnp.transpose(g_t).astype(BF16)

    quarter = half // 2

    def blocks(side):
        limit = top if side == 0 else keys
        return [(low, low + quarter) for low in range(0, limit, quarter)]

    def column(side):
        return slice(side * half, (side + 1) * half)

    def fold(x):
        return jnp.sum(x.reshape(-1, 8, half), axis=0)

    def exponentials(slot, side):
        s_ref, d_ref, m_ref = slot[0], slot[1], slot[4]
        cols = column(side)
        m = m_ref[:, cols]
        norm = jnp.zeros((8, half), F32)
        dots = jnp.zeros((8, half), F32)
        for low, high in blocks(side):
            e = jnp.exp2(s_ref[low:high, cols] * to_exp2 - m)
            s_ref[low:high, cols] = e
            norm = norm + fold(e)
            dots = dots + fold(e * d_ref[low:high, cols])
        inv = 1.0 / jnp.sum(norm, axis=0, keepdims=True)
        return inv, jnp.sum(dots, axis=0, keepdims=True) * inv

    def differences(slot, side, inv, dot_row):
        s_ref, d_ref, p_ref, ds_ref = slot[:4]
        cols = column(side)
        for low, high in blocks(side):
            p = s_ref[low:high, cols] * inv
            p_ref[low:high, cols] = p.astype(BF16)
            ds_ref[low:high, cols] = (p * (d_ref[low:high, cols] - dot_row)).astype(BF16)

    def step(head, cur, other):
        ahead = jnp.minimum(head + 1, heads - 1)
        behind = jnp.maximum(head - 1, 0)
        scores(ahead, other)
        stats_0 = exponentials(cur, 0)
        add_key_grad(behind, other)
        stats_1 = exponentials(cur, 1)
        add_value_grad(behind, other)
        differences(cur, 0, *stats_0)
        query_grad(behind, other)
        differences(cur, 1, *stats_1)
        value_products(ahead, other)

    def send_sums(kv):
        grad_k = gk_acc[kv] * scaling
        grad_v = gv_acc[kv]
        sa[kv, :, 0] = grad_k[:plen].astype(BF16).reshape(n_r, rows, HD)
        sa[kv, :, 1] = grad_v[:plen].astype(BF16).reshape(n_r, rows, HD)
        for i in range(1, n_r):
            sum_first(kv, row_peer(i), r).start()
        ra[kv, r] = sa[kv, r]
        lanes = head_lanes(kv)
        grk_ref[0, :, lanes] = grad_k[plen:].astype(BF16)
        grv_ref[0, :, lanes] = grad_v[plen:].astype(BF16)
        store_queries(kv).start()

    def store_queries(kv):
        cols = pl.ds(pl.multiple_of(kv * GRP * HD, HD), GRP * HD)
        return pltpu.make_async_copy(gq_v.at[:, cols], gq_out.at[0, :, cols], out_sem.at[kv])

    def combine(kv):
        for i in range(1, n_r):
            sum_first(kv, row_peer(i), row_peer(i)).wait_recv()
        sums = [jnp.zeros((2, rows, HD), F32) for _ in range(n_p)]
        for src in range(n_r):
            owner = prompt_of(src)
            term = ra[kv, src].astype(F32)
            for p in range(n_p):
                sums[p] = sums[p] + jnp.where(owner == p, term, 0.0)
        for p in range(n_p):
            sb[kv, p] = sums[p]
        for i in range(1, n_p):
            sum_second(kv, column_peer(i), c).start()

    def finish(kv):
        lanes = head_lanes(kv)
        out = sb[kv, c]
        for i in range(1, n_p):
            sum_second(kv, column_peer(i), column_peer(i)).wait_recv()
            out = out + rb[kv, column_peer(i)]
        gpk_ref[0, :, lanes] = out[0]
        gpv_ref[0, :, lanes] = out[1]

    load_keys(jnp.int32(0))
    scores(0, slots[0])
    value_products(0, slots[0])
    pairs = GRP // 2

    def pair(index, carry):
        kv = index // pairs
        place = index % pairs

        @pl.when((place == pairs - 1) & (kv < kv_heads - 1))
        def _():
            load_keys(kv + 1)

        @pl.when((place == 1) & (kv > 0))
        def _():
            send_sums(kv - 1)

        @pl.when((place == pairs - 1) & (kv > 0))
        def _():
            combine(kv - 1)

        step(2 * index, slots[0], slots[1])
        step(2 * index + 1, slots[1], slots[0])
        return carry

    lax.fori_loop(0, heads // 2, pair, 0)
    add_key_grad(heads - 1, slots[1])
    add_value_grad(heads - 1, slots[1])
    query_grad(heads - 1, slots[1])
    send_sums(kv_heads - 1)
    for kv in range(kv_heads - 1):
        finish(kv)
    combine(kv_heads - 1)
    finish(kv_heads - 1)

    for kv in range(kv_heads):
        store_queries(kv).wait()
        for i in range(1, n_p):
            gather_first(kv, column_peer(i), c).wait_send()
        for i in range(1, n_r):
            gather_second(kv, row_peer(i), r).wait_send()
            sum_first(kv, row_peer(i), r).wait_send()
        for i in range(1, n_p):
            sum_second(kv, column_peer(i), c).wait_send()


def store_kernel(pieces, *refs):
    count = len(pieces)
    sources, targets, staged = refs[:count], refs[count : 2 * count], refs[2 * count : 3 * count]
    in_sem, out_sem = refs[3 * count :]
    loads, stores = [], []
    for k, parts in enumerate(pieces):
        size = sources[k].shape[1] // parts
        for part in range(parts):
            rows = pl.ds(part * size, size)
            place = len(loads)
            loads.append(
                pltpu.make_async_copy(
                    sources[k].at[:, rows], staged[k].at[:, rows], in_sem.at[place]
                )
            )
            stores.append(
                pltpu.make_async_copy(
                    staged[k].at[:, rows], targets[k].at[:, rows], out_sem.at[place]
                )
            )
    for load in loads:
        load.start()
    for load, store in zip(loads, stores):
        load.wait()
        store.start()
    for store in stores:
        store.wait()


def per_device(
    queries,
    resp_keys,
    resp_values,
    grad_out,
    prompt_keys,
    prompt_values,
    group_sizes,
    slot_response,
    lengths,
):
    n_p = lax.axis_size("prompt")
    n_r = lax.axis_size("resp")
    tok = queries.shape[1]
    width = queries.shape[2]
    rows = prompt_keys.shape[1]
    kv_width = prompt_keys.shape[2]
    kv_heads = kv_width // HD
    keys = rows * n_r + tok
    vmem = pl.BlockSpec(memory_space=pltpu.VMEM)
    hbm = pl.BlockSpec(memory_space=pltpu.HBM)
    anywhere = pl.BlockSpec(memory_space=pl.ANY)
    dma = pltpu.SemaphoreType.DMA
    out_shape = (
        jax.ShapeDtypeStruct(queries.shape, BF16),
        jax.ShapeDtypeStruct(resp_keys.shape, BF16),
        jax.ShapeDtypeStruct(resp_values.shape, BF16),
        jax.ShapeDtypeStruct(prompt_keys.shape, F32),
        jax.ShapeDtypeStruct(prompt_values.shape, F32),
    )
    results = pl.pallas_call(
        functools.partial(kernel, n_p, n_r),
        out_shape=out_shape,
        in_specs=[hbm] * 9,
        out_specs=(anywhere, vmem, vmem, vmem, vmem),
        scratch_shapes=[
            pltpu.VMEM((tok, width), BF16),
            pltpu.VMEM((tok, width), BF16),
            pltpu.VMEM((tok, width), BF16),
            pltpu.SMEM(group_sizes.shape, jnp.int32),
            pltpu.SMEM(slot_response.shape, jnp.int32),
            pltpu.SMEM(lengths.shape, jnp.int32),
            pltpu.VMEM((2, rows, kv_width), BF16),
            pltpu.VMEM((kv_heads, n_p, 2, rows, HD), BF16),
            pltpu.VMEM((kv_heads, n_r, 2, rows, HD), BF16),
            pltpu.VMEM((kv_heads, n_r, 2, rows, HD), BF16),
            pltpu.VMEM((kv_heads, n_r, 2, rows, HD), BF16),
            pltpu.VMEM((kv_heads, n_r, 2, rows, HD), BF16),
            pltpu.VMEM((kv_heads, n_p, 2, rows, HD), F32),
            pltpu.VMEM((kv_heads, n_p, 2, rows, HD), F32),
            pltpu.VMEM((kv_heads, keys, HD), BF16),
            pltpu.VMEM((kv_heads, keys, HD), BF16),
            pltpu.VMEM((kv_heads, HD, keys), BF16),
            pltpu.VMEM((kv_heads, keys, HD), F32),
            pltpu.VMEM((kv_heads, keys, HD), F32),
            pltpu.VMEM((keys, tok), F32),
            pltpu.VMEM((keys, tok), F32),
            pltpu.VMEM((keys, tok), F32),
            pltpu.VMEM((keys, tok), F32),
            pltpu.VMEM((keys, tok), BF16),
            pltpu.VMEM((keys, tok), BF16),
            pltpu.VMEM((keys, tok), BF16),
            pltpu.VMEM((keys, tok), BF16),
            pltpu.VMEM((1, tok), F32),
            pltpu.VMEM((1, tok), F32),
            dma((7,)),
            dma((2, kv_heads)),
            dma((kv_heads,)),
            dma((kv_heads, n_p)),
            dma((kv_heads, n_p)),
            dma((kv_heads, n_r)),
            dma((kv_heads, n_r)),
            dma((kv_heads, n_r)),
            dma((kv_heads, n_r)),
            dma((kv_heads, n_p)),
            dma((kv_heads, n_p)),
        ],
        compiler_params=pltpu.CompilerParams(
            collective_id=0, has_side_effects=True, vmem_limit_bytes=VMEM_LIMIT
        ),
        cost_estimate=pl.CostEstimate(
            flops=10 * tok * keys * width,
            bytes_accessed=4 * tok * width * 2,
            transcendentals=tok * keys * width // HD,
        ),
    )(
        queries,
        grad_out,
        resp_keys,
        resp_values,
        prompt_keys,
        prompt_values,
        group_sizes,
        slot_response,
        lengths,
    )
    pieces = (4, 1, 1, 1, 1)
    return pl.pallas_call(
        functools.partial(store_kernel, pieces),
        out_shape=out_shape,
        in_specs=[hbm] * len(out_shape),
        out_specs=(hbm,) * len(out_shape),
        scratch_shapes=[pltpu.VMEM(out.shape, out.dtype) for out in out_shape]
        + [dma((sum(pieces),)), dma((sum(pieces),))],
        compiler_params=pltpu.CompilerParams(vmem_limit_bytes=VMEM_LIMIT),
    )(*results)


def solution(mesh):
    in_specs = (
        P(("prompt", "resp"), None, None),
        P(("prompt", "resp"), None, None),
        P(("prompt", "resp"), None, None),
        P(("prompt", "resp"), None, None),
        P("prompt", "resp", None),
        P("prompt", "resp", None),
        P(),
        P(),
        P(("prompt", "resp")),
    )
    out_specs = (
        P(("prompt", "resp"), None, None),
        P(("prompt", "resp"), None, None),
        P(("prompt", "resp"), None, None),
        P("prompt", "resp", None),
        P("prompt", "resp", None),
    )
    return jax.shard_map(
        per_device, mesh=mesh, in_specs=in_specs, out_specs=out_specs, check_vma=False
    )
```

```python
import functools
import math

import jax
import jax.numpy as jnp
from jax import lax
from jax.experimental import pallas as pl
from jax.experimental.pallas import tpu as pltpu
from jax.sharding import PartitionSpec as P

HD = 128
GRP = 8
VMEM_LIMIT = 60 * 1024 * 1024
MESH = pl.DeviceIdType.MESH
F32 = jnp.float32
BF16 = jnp.bfloat16


def nt(a, b):
    return lax.dot_general(a, b, (((1,), (1,)), ((), ())), preferred_element_type=F32)


def nn(a, b):
    return jnp.dot(a, b, preferred_element_type=F32)


def kernel(
    n_p,
    n_r,
    q_hbm,
    do_hbm,
    rk_hbm,
    rv_hbm,
    pk_hbm,
    pv_hbm,
    sizes_hbm,
    slot_hbm,
    len_hbm,
    gq_out,
    grk_ref,
    grv_ref,
    gpk_ref,
    gpv_ref,
    q_v,
    do_v,
    gq_v,
    sizes_ref,
    slot_ref,
    len_ref,
    own,
    g1,
    s2,
    r2,
    sa,
    ra,
    sb,
    rb,
    kall,
    vall,
    ktall,
    gk_acc,
    gv_acc,
    s_0,
    s_1,
    d_0,
    d_1,
    p_0,
    p_1,
    ds_0,
    ds_1,
    m_0,
    m_1,
    in_sem,
    kv_sem,
    out_sem,
    g1_send,
    g1_recv,
    s2_send,
    s2_recv,
    a_send,
    a_recv,
    b_send,
    b_recv,
):
    c = lax.axis_index("prompt")
    r = lax.axis_index("resp")
    rows = g1.shape[3]
    kv_heads = kall.shape[0]
    heads = kv_heads * GRP
    tok = q_v.shape[0]
    plen = rows * n_r
    half = tok // 2
    top = plen + half
    keys = plen + tok
    scaling = 1.0 / math.sqrt(HD)
    to_exp2 = scaling * math.log2(math.e)

    def column_peer(i):
        return lax.rem(c + i, n_p)

    def row_peer(i):
        return lax.rem(r + i, n_r)

    def prompt_of(resp_index):
        value = slot_ref[c * n_r + resp_index]
        end = sizes_ref[0]
        found = (value >= end).astype(jnp.int32)
        for k in range(1, n_p - 1):
            end = end + sizes_ref[k]
            found = found + (value >= end).astype(jnp.int32)
        return found

    first = [
        pltpu.make_async_copy(pk_hbm.at[0], own.at[0], in_sem.at[0]),
        pltpu.make_async_copy(pv_hbm.at[0], own.at[1], in_sem.at[1]),
        pltpu.make_async_copy(sizes_hbm, sizes_ref, in_sem.at[2]),
        pltpu.make_async_copy(slot_hbm, slot_ref, in_sem.at[3]),
        pltpu.make_async_copy(len_hbm, len_ref, in_sem.at[4]),
    ]
    q_in = pltpu.make_async_copy(q_hbm.at[0], q_v, in_sem.at[5])
    do_in = pltpu.make_async_copy(do_hbm.at[0], do_v, in_sem.at[6])
    resp_in = []
    for kv in range(kv_heads):
        lanes = pl.ds(kv * HD, HD)
        resp_in.append(
            pltpu.make_async_copy(
                rk_hbm.at[0, :, lanes], kall.at[kv, pl.ds(plen, tok)], kv_sem.at[0, kv]
            )
        )
        resp_in.append(
            pltpu.make_async_copy(
                rv_hbm.at[0, :, lanes], vall.at[kv, pl.ds(plen, tok)], kv_sem.at[1, kv]
            )
        )
    for copy in first + [do_in, q_in] + resp_in:
        copy.start()

    barrier = pltpu.get_barrier_semaphore()
    for i in range(1, n_p):
        pl.semaphore_signal(barrier, inc=1, device_id=(column_peer(i), r), device_id_type=MESH)
    for i in range(1, n_r):
        pl.semaphore_signal(barrier, inc=1, device_id=(c, row_peer(i)), device_id_type=MESH)
    for copy in first:
        copy.wait()
    for kv in range(kv_heads):
        g1[kv, c] = own[:, :, kv * HD : (kv + 1) * HD]
    pl.semaphore_wait(barrier, n_p + n_r - 2)

    def gather_first(kv, to, slot):
        return pltpu.make_async_remote_copy(
            src_ref=g1.at[kv, slot],
            dst_ref=g1.at[kv, slot],
            send_sem=g1_send.at[kv, to],
            recv_sem=g1_recv.at[kv, slot],
            device_id=(to, r),
            device_id_type=MESH,
        )

    def gather_second(kv, to, slot):
        return pltpu.make_async_remote_copy(
            src_ref=s2.at[kv, to],
            dst_ref=r2.at[kv, slot],
            send_sem=s2_send.at[kv, to],
            recv_sem=s2_recv.at[kv, slot],
            device_id=(c, to),
            device_id_type=MESH,
        )

    def sum_first(kv, to, slot):
        return pltpu.make_async_remote_copy(
            src_ref=sa.at[kv, to],
            dst_ref=ra.at[kv, slot],
            send_sem=a_send.at[kv, to],
            recv_sem=a_recv.at[kv, slot],
            device_id=(c, to),
            device_id_type=MESH,
        )

    def sum_second(kv, to, slot):
        return pltpu.make_async_remote_copy(
            src_ref=sb.at[kv, to],
            dst_ref=rb.at[kv, slot],
            send_sem=b_send.at[kv, to],
            recv_sem=b_recv.at[kv, slot],
            device_id=(to, r),
            device_id_type=MESH,
        )

    def send_first(kv):
        for i in range(1, n_p):
            gather_first(kv, column_peer(i), c).start()

    def picked(kv, to):
        owner = prompt_of(to)
        block = g1[kv, 0]
        for p in range(1, n_p):
            block = jnp.where(owner == p, g1[kv, p], block)
        return block

    def send_second(kv):
        for i in range(1, n_p):
            gather_first(kv, column_peer(i), column_peer(i)).wait_recv()
        for i in range(1, n_r):
            to = row_peer(i)
            s2[kv, to] = picked(kv, to)
            gather_second(kv, to, r).start()
        r2[kv, r] = picked(kv, r)

    send_first(0)
    send_second(0)
    for kv in range(1, kv_heads):
        send_first(kv)
    gk_acc[...] = jnp.zeros_like(gk_acc)
    gv_acc[...] = jnp.zeros_like(gv_acc)
    for ref in (p_0, p_1, ds_0, ds_1):
        ref[...] = jnp.zeros_like(ref)
    do_in.wait()
    live_mask = lax.broadcasted_iota(jnp.int32, (tok, HD), 0) < len_ref[0]

    def mask_rows(head, carry):
        lanes = pl.ds(pl.multiple_of(head * HD, HD), HD)
        do_v[:, lanes] = jnp.where(live_mask, do_v[:, lanes], jnp.zeros((), BF16))
        return carry

    lax.fori_loop(0, heads, mask_rows, 0)
    q_in.wait()
    for copy in resp_in:
        copy.wait()

    slots = ((s_0, d_0, p_0, ds_0, m_0), (s_1, d_1, p_1, ds_1, m_1))

    def head_lanes(head):
        return pl.ds(pl.multiple_of(head * HD, HD), HD)

    def load_keys(kv):
        for i in range(1, n_r):
            gather_second(kv, row_peer(i), row_peer(i)).wait_recv()
        kall[kv, :plen] = r2[kv, :, 0].reshape(plen, HD)
        vall[kv, :plen] = r2[kv, :, 1].reshape(plen, HD)
        ktall[kv] = jnp.transpose(kall[kv].astype(F32)).astype(BF16)

    def scores(head, slot):
        s_ref, m_ref = slot[0], slot[4]
        s = nt(kall[head // GRP], q_v[:, head_lanes(head)])
        causal = lax.broadcasted_iota(jnp.int32, (half, half), 0) <= lax.broadcasted_iota(
            jnp.int32, (half, half), 1
        )
        s_p = s[:plen]
        s_l = jnp.where(causal, s[plen:top, :half], -jnp.inf)
        s_r = s[plen:top, half:]
        s_b = jnp.where(causal, s[top:, half:], -jnp.inf)
        s_ref[:plen] = s_p
        s_ref[plen:top, :half] = s_l
        s_ref[plen:top, half:] = s_r
        s_ref[top:, half:] = s_b
        m_p = jnp.max(s_p, axis=0, keepdims=True)
        m_l = jnp.max(s_l, axis=0, keepdims=True)
        m_r = jnp.max(jnp.maximum(s_r, s_b), axis=0, keepdims=True)
        m_ref[...] = jnp.maximum(m_p, jnp.concatenate([m_l, m_r], axis=1)) * to_exp2

    def value_products(head, slot):
        slot[1][...] = nt(vall[head // GRP], do_v[:, head_lanes(head)])

    def add_key_grad(head, slot):
        gk_acc[head // GRP] += nn(slot[3][...], q_v[:, head_lanes(head)])

    def add_value_grad(head, slot):
        gv_acc[head // GRP] += nn(slot[2][...], do_v[:, head_lanes(head)])

    def query_grad(head, slot):
        g_t = nn(ktall[head // GRP], slot[3][...]) * scaling
        gq_v[:, head_lanes(head)] = jnp.transpose(g_t).astype(BF16)

    quarter = half // 2

    def blocks(side):
        limit = top if side == 0 else keys
        return [(low, low + quarter) for low in range(0, limit, quarter)]

    def column(side):
        return slice(side * half, (side + 1) * half)

    def fold(x):
        return jnp.sum(x.reshape(-1, 8, half), axis=0)

    def exponentials(slot, side):
        s_ref, d_ref, m_ref = slot[0], slot[1], slot[4]
        cols = column(side)
        m = m_ref[:, cols]
        norm = jnp.zeros((8, half), F32)
        dots = jnp.zeros((8, half), F32)
        for low, high in blocks(side):
            e = jnp.exp2(s_ref[low:high, cols] * to_exp2 - m)
            s_ref[low:high, cols] = e
            norm = norm + fold(e)
            dots = dots + fold(e * d_ref[low:high, cols])
        inv = 1.0 / jnp.sum(norm, axis=0, keepdims=True)
        return inv, jnp.sum(dots, axis=0, keepdims=True) * inv

    def differences(slot, side, inv, dot_row):
        s_ref, d_ref, p_ref, ds_ref = slot[:4]
        cols = column(side)
        for low, high in blocks(side):
            p = s_ref[low:high, cols] * inv
            p_ref[low:high, cols] = p.astype(BF16)
            ds_ref[low:high, cols] = (p * (d_ref[low:high, cols] - dot_row)).astype(BF16)

    def step(head, cur, other):
        ahead = jnp.minimum(head + 1, heads - 1)
        behind = jnp.maximum(head - 1, 0)
        scores(ahead, other)
        stats_0 = exponentials(cur, 0)
        add_key_grad(behind, other)
        stats_1 = exponentials(cur, 1)
        add_value_grad(behind, other)
        differences(cur, 0, *stats_0)
        query_grad(behind, other)
        differences(cur, 1, *stats_1)
        value_products(ahead, other)

    def send_sums(kv):
        grad_k = gk_acc[kv] * scaling
        grad_v = gv_acc[kv]
        sa[kv, :, 0] = grad_k[:plen].astype(BF16).reshape(n_r, rows, HD)
        sa[kv, :, 1] = grad_v[:plen].astype(BF16).reshape(n_r, rows, HD)
        for i in range(1, n_r):
            sum_first(kv, row_peer(i), r).start()
        ra[kv, r] = sa[kv, r]
        lanes = head_lanes(kv)
        grk_ref[0, :, lanes] = grad_k[plen:].astype(BF16)
        grv_ref[0, :, lanes] = grad_v[plen:].astype(BF16)
        store_queries(kv).start()

    def store_queries(kv):
        cols = pl.ds(pl.multiple_of(kv * GRP * HD, HD), GRP * HD)
        return pltpu.make_async_copy(gq_v.at[:, cols], gq_out.at[0, :, cols], out_sem.at[kv])

    def combine(kv):
        for i in range(1, n_r):
            sum_first(kv, row_peer(i), row_peer(i)).wait_recv()
        sums = [jnp.zeros((2, rows, HD), F32) for _ in range(n_p)]
        for src in range(n_r):
            owner = prompt_of(src)
            term = ra[kv, src].astype(F32)
            for p in range(n_p):
                sums[p] = sums[p] + jnp.where(owner == p, term, 0.0)
        for p in range(n_p):
            sb[kv, p] = sums[p]
        for i in range(1, n_p):
            sum_second(kv, column_peer(i), c).start()

    def finish(kv):
        lanes = head_lanes(kv)
        out = sb[kv, c]
        for i in range(1, n_p):
            sum_second(kv, column_peer(i), column_peer(i)).wait_recv()
            out = out + rb[kv, column_peer(i)]
        gpk_ref[0, :, lanes] = out[0]
        gpv_ref[0, :, lanes] = out[1]

    load_keys(0)
    if kv_heads > 1:
        send_second(1)
    scores(0, slots[0])
    value_products(0, slots[0])
    pairs = GRP // 2

    def pair(index, carry):
        kv = index // pairs
        place = index % pairs

        @pl.when((place == pairs - 1) & (kv < kv_heads - 1))
        def _():
            load_keys(kv + 1)

        @pl.when((place == 1) & (kv > 0))
        def _():
            send_sums(kv - 1)

        @pl.when((place == 1) & (kv > 1))
        def _():
            combine(kv - 2)

        @pl.when((place == 2) & (kv < kv_heads - 2))
        def _():
            send_second(kv + 2)

        step(2 * index, slots[0], slots[1])
        step(2 * index + 1, slots[1], slots[0])
        return carry

    lax.fori_loop(0, heads // 2, pair, 0)
    add_key_grad(heads - 1, slots[1])
    add_value_grad(heads - 1, slots[1])
    query_grad(heads - 1, slots[1])
    send_sums(kv_heads - 1)
    if kv_heads > 1:
        combine(kv_heads - 2)
    for kv in range(kv_heads - 2):
        finish(kv)
    combine(kv_heads - 1)
    for kv in range(max(kv_heads - 2, 0), kv_heads):
        finish(kv)

    for kv in range(kv_heads):
        store_queries(kv).wait()
        for i in range(1, n_p):
            gather_first(kv, column_peer(i), c).wait_send()
        for i in range(1, n_r):
            gather_second(kv, row_peer(i), r).wait_send()
            sum_first(kv, row_peer(i), r).wait_send()
        for i in range(1, n_p):
            sum_second(kv, column_peer(i), c).wait_send()


def store_kernel(pieces, *refs):
    count = len(pieces)
    sources, targets, staged = refs[:count], refs[count : 2 * count], refs[2 * count : 3 * count]
    in_sem, out_sem = refs[3 * count :]
    loads, stores = [], []
    for k, parts in enumerate(pieces):
        size = sources[k].shape[1] // parts
        for part in range(parts):
            rows = pl.ds(part * size, size)
            place = len(loads)
            loads.append(
                pltpu.make_async_copy(
                    sources[k].at[:, rows], staged[k].at[:, rows], in_sem.at[place]
                )
            )
            stores.append(
                pltpu.make_async_copy(
                    staged[k].at[:, rows], targets[k].at[:, rows], out_sem.at[place]
                )
            )
    for load in loads:
        load.start()
    for load, store in zip(loads, stores):
        load.wait()
        store.start()
    for store in stores:
        store.wait()


def per_device(
    queries,
    resp_keys,
    resp_values,
    grad_out,
    prompt_keys,
    prompt_values,
    group_sizes,
    slot_response,
    lengths,
):
    n_p = lax.axis_size("prompt")
    n_r = lax.axis_size("resp")
    tok = queries.shape[1]
    width = queries.shape[2]
    rows = prompt_keys.shape[1]
    kv_width = prompt_keys.shape[2]
    kv_heads = kv_width // HD
    keys = rows * n_r + tok
    vmem = pl.BlockSpec(memory_space=pltpu.VMEM)
    hbm = pl.BlockSpec(memory_space=pltpu.HBM)
    anywhere = pl.BlockSpec(memory_space=pl.ANY)
    dma = pltpu.SemaphoreType.DMA
    out_shape = (
        jax.ShapeDtypeStruct(queries.shape, BF16),
        jax.ShapeDtypeStruct(resp_keys.shape, BF16),
        jax.ShapeDtypeStruct(resp_values.shape, BF16),
        jax.ShapeDtypeStruct(prompt_keys.shape, F32),
        jax.ShapeDtypeStruct(prompt_values.shape, F32),
    )
    results = pl.pallas_call(
        functools.partial(kernel, n_p, n_r),
        out_shape=out_shape,
        in_specs=[hbm] * 9,
        out_specs=(anywhere, vmem, vmem, vmem, vmem),
        scratch_shapes=[
            pltpu.VMEM((tok, width), BF16),
            pltpu.VMEM((tok, width), BF16),
            pltpu.VMEM((tok, width), BF16),
            pltpu.SMEM(group_sizes.shape, jnp.int32),
            pltpu.SMEM(slot_response.shape, jnp.int32),
            pltpu.SMEM(lengths.shape, jnp.int32),
            pltpu.VMEM((2, rows, kv_width), BF16),
            pltpu.VMEM((kv_heads, n_p, 2, rows, HD), BF16),
            pltpu.VMEM((kv_heads, n_r, 2, rows, HD), BF16),
            pltpu.VMEM((kv_heads, n_r, 2, rows, HD), BF16),
            pltpu.VMEM((kv_heads, n_r, 2, rows, HD), BF16),
            pltpu.VMEM((kv_heads, n_r, 2, rows, HD), BF16),
            pltpu.VMEM((kv_heads, n_p, 2, rows, HD), F32),
            pltpu.VMEM((kv_heads, n_p, 2, rows, HD), F32),
            pltpu.VMEM((kv_heads, keys, HD), BF16),
            pltpu.VMEM((kv_heads, keys, HD), BF16),
            pltpu.VMEM((kv_heads, HD, keys), BF16),
            pltpu.VMEM((kv_heads, keys, HD), F32),
            pltpu.VMEM((kv_heads, keys, HD), F32),
            pltpu.VMEM((keys, tok), F32),
            pltpu.VMEM((keys, tok), F32),
            pltpu.VMEM((keys, tok), F32),
            pltpu.VMEM((keys, tok), F32),
            pltpu.VMEM((keys, tok), BF16),
            pltpu.VMEM((keys, tok), BF16),
            pltpu.VMEM((keys, tok), BF16),
            pltpu.VMEM((keys, tok), BF16),
            pltpu.VMEM((1, tok), F32),
            pltpu.VMEM((1, tok), F32),
            dma((7,)),
            dma((2, kv_heads)),
            dma((kv_heads,)),
            dma((kv_heads, n_p)),
            dma((kv_heads, n_p)),
            dma((kv_heads, n_r)),
            dma((kv_heads, n_r)),
            dma((kv_heads, n_r)),
            dma((kv_heads, n_r)),
            dma((kv_heads, n_p)),
            dma((kv_heads, n_p)),
        ],
        compiler_params=pltpu.CompilerParams(
            collective_id=0, has_side_effects=True, vmem_limit_bytes=VMEM_LIMIT
        ),
        cost_estimate=pl.CostEstimate(
            flops=10 * tok * keys * width,
            bytes_accessed=4 * tok * width * 2,
            transcendentals=tok * keys * width // HD,
        ),
    )(
        queries,
        grad_out,
        resp_keys,
        resp_values,
        prompt_keys,
        prompt_values,
        group_sizes,
        slot_response,
        lengths,
    )
    pieces = (4, 1, 1, 1, 1)
    return pl.pallas_call(
        functools.partial(store_kernel, pieces),
        out_shape=out_shape,
        in_specs=[hbm] * len(out_shape),
        out_specs=(hbm,) * len(out_shape),
        scratch_shapes=[pltpu.VMEM(out.shape, out.dtype) for out in out_shape]
        + [dma((sum(pieces),)), dma((sum(pieces),))],
        compiler_params=pltpu.CompilerParams(vmem_limit_bytes=VMEM_LIMIT),
    )(*results)


def solution(mesh):
    in_specs = (
        P(("prompt", "resp"), None, None),
        P(("prompt", "resp"), None, None),
        P(("prompt", "resp"), None, None),
        P(("prompt", "resp"), None, None),
        P("prompt", "resp", None),
        P("prompt", "resp", None),
        P(),
        P(),
        P(("prompt", "resp")),
    )
    out_specs = (
        P(("prompt", "resp"), None, None),
        P(("prompt", "resp"), None, None),
        P(("prompt", "resp"), None, None),
        P("prompt", "resp", None),
        P("prompt", "resp", None),
    )
    return jax.shard_map(
        per_device, mesh=mesh, in_specs=in_specs, out_specs=out_specs, check_vma=False
    )
```

```python
import functools
import math

import jax
import jax.numpy as jnp
from jax import lax
from jax.experimental import pallas as pl
from jax.experimental.pallas import tpu as pltpu
from jax.sharding import PartitionSpec as P

HD = 128
GRP = 8
VMEM_LIMIT = 60 * 1024 * 1024
MESH = pl.DeviceIdType.MESH
F32 = jnp.float32
BF16 = jnp.bfloat16


def nt(a, b):
    return lax.dot_general(a, b, (((1,), (1,)), ((), ())), preferred_element_type=F32)


def nn(a, b):
    return jnp.dot(a, b, preferred_element_type=F32)


def kernel(
    n_p,
    n_r,
    q_hbm,
    do_hbm,
    rk_hbm,
    rv_hbm,
    pk_hbm,
    pv_hbm,
    sizes_hbm,
    slot_hbm,
    len_hbm,
    gq_out,
    grk_ref,
    grv_ref,
    gpk_ref,
    gpv_ref,
    q_v,
    do_v,
    gq_v,
    sizes_ref,
    slot_ref,
    len_ref,
    own,
    g1,
    s2,
    r2,
    sa,
    ra,
    kept,
    sb,
    rb,
    kall,
    vall,
    ktall,
    gk_acc,
    gv_acc,
    s_0,
    s_1,
    d_0,
    d_1,
    p_0,
    p_1,
    ds_0,
    ds_1,
    m_0,
    m_1,
    in_sem,
    kv_sem,
    out_sem,
    g1_send,
    g1_recv,
    s2_send,
    s2_recv,
    a_send,
    a_recv,
    b_send,
    b_recv,
):
    c = lax.axis_index("prompt")
    r = lax.axis_index("resp")
    rows = g1.shape[3]
    kv_heads = kall.shape[0]
    heads = kv_heads * GRP
    tok = q_v.shape[0]
    plen = rows * n_r
    half = tok // 2
    top = plen + half
    keys = plen + tok
    scaling = 1.0 / math.sqrt(HD)
    to_exp2 = scaling * math.log2(math.e)

    def column_peer(i):
        return lax.rem(c + i, n_p)

    def row_peer(i):
        return lax.rem(r + i, n_r)

    def prompt_of(resp_index):
        value = slot_ref[c * n_r + resp_index]
        end = sizes_ref[0]
        found = (value >= end).astype(jnp.int32)
        for k in range(1, n_p - 1):
            end = end + sizes_ref[k]
            found = found + (value >= end).astype(jnp.int32)
        return found

    first = [
        pltpu.make_async_copy(pk_hbm.at[0], own.at[0], in_sem.at[0]),
        pltpu.make_async_copy(pv_hbm.at[0], own.at[1], in_sem.at[1]),
        pltpu.make_async_copy(sizes_hbm, sizes_ref, in_sem.at[2]),
        pltpu.make_async_copy(slot_hbm, slot_ref, in_sem.at[3]),
        pltpu.make_async_copy(len_hbm, len_ref, in_sem.at[4]),
    ]
    q_in = pltpu.make_async_copy(q_hbm.at[0], q_v, in_sem.at[5])
    do_in = pltpu.make_async_copy(do_hbm.at[0], do_v, in_sem.at[6])
    resp_in = []
    for kv in range(kv_heads):
        lanes = pl.ds(kv * HD, HD)
        resp_in.append(
            pltpu.make_async_copy(
                rk_hbm.at[0, :, lanes], kall.at[kv, pl.ds(plen, tok)], kv_sem.at[0, kv]
            )
        )
        resp_in.append(
            pltpu.make_async_copy(
                rv_hbm.at[0, :, lanes], vall.at[kv, pl.ds(plen, tok)], kv_sem.at[1, kv]
            )
        )
    for copy in first + [do_in, q_in] + resp_in:
        copy.start()

    barrier = pltpu.get_barrier_semaphore()
    for i in range(1, n_p):
        pl.semaphore_signal(barrier, inc=1, device_id=(column_peer(i), r), device_id_type=MESH)
    for i in range(1, n_r):
        pl.semaphore_signal(barrier, inc=1, device_id=(c, row_peer(i)), device_id_type=MESH)
    for copy in first:
        copy.wait()
    for kv in range(kv_heads):
        g1[kv, c] = own[:, :, kv * HD : (kv + 1) * HD]
    pl.semaphore_wait(barrier, n_p + n_r - 2)

    def gather_first(kv, to, slot):
        return pltpu.make_async_remote_copy(
            src_ref=g1.at[kv, slot],
            dst_ref=g1.at[kv, slot],
            send_sem=g1_send.at[kv, to],
            recv_sem=g1_recv.at[kv, slot],
            device_id=(to, r),
            device_id_type=MESH,
        )

    def gather_second(kv, to, slot):
        return pltpu.make_async_remote_copy(
            src_ref=s2.at[kv, to],
            dst_ref=r2.at[kv, slot],
            send_sem=s2_send.at[kv, to],
            recv_sem=s2_recv.at[kv, slot],
            device_id=(c, to),
            device_id_type=MESH,
        )

    def sum_first(kv, to, slot):
        return pltpu.make_async_remote_copy(
            src_ref=sa.at[kv, to],
            dst_ref=ra.at[kv, slot],
            send_sem=a_send.at[kv, to],
            recv_sem=a_recv.at[kv, slot],
            device_id=(c, to),
            device_id_type=MESH,
        )

    def sum_second(kv, to, slot):
        return pltpu.make_async_remote_copy(
            src_ref=sb.at[kv, to],
            dst_ref=rb.at[kv, slot],
            send_sem=b_send.at[kv, to],
            recv_sem=b_recv.at[kv, slot],
            device_id=(to, r),
            device_id_type=MESH,
        )

    def send_first(kv):
        for i in range(1, n_p):
            gather_first(kv, column_peer(i), c).start()

    def picked(kv, to):
        owner = prompt_of(to)
        block = g1[kv, 0]
        for p in range(1, n_p):
            block = jnp.where(owner == p, g1[kv, p], block)
        return block

    def send_second(kv):
        for i in range(1, n_p):
            gather_first(kv, column_peer(i), column_peer(i)).wait_recv()
        for i in range(1, n_r):
            to = row_peer(i)
            s2[kv, to] = picked(kv, to)
            gather_second(kv, to, r).start()
        r2[kv, r] = picked(kv, r)

    send_first(0)
    send_second(0)
    for kv in range(1, kv_heads):
        send_first(kv)
    gk_acc[...] = jnp.zeros_like(gk_acc)
    gv_acc[...] = jnp.zeros_like(gv_acc)
    for ref in (p_0, p_1, ds_0, ds_1):
        ref[...] = jnp.zeros_like(ref)
    do_in.wait()
    live_mask = lax.broadcasted_iota(jnp.int32, (tok, HD), 0) < len_ref[0]

    def mask_rows(head, carry):
        lanes = pl.ds(pl.multiple_of(head * HD, HD), HD)
        do_v[:, lanes] = jnp.where(live_mask, do_v[:, lanes], jnp.zeros((), BF16))
        return carry

    lax.fori_loop(0, heads, mask_rows, 0)
    q_in.wait()
    for copy in resp_in:
        copy.wait()

    slots = ((s_0, d_0, p_0, ds_0, m_0), (s_1, d_1, p_1, ds_1, m_1))

    def head_lanes(head):
        return pl.ds(pl.multiple_of(head * HD, HD), HD)

    def load_keys(kv):
        for i in range(1, n_r):
            gather_second(kv, row_peer(i), row_peer(i)).wait_recv()
        kall[kv, :plen] = r2[kv, :, 0].reshape(plen, HD)
        vall[kv, :plen] = r2[kv, :, 1].reshape(plen, HD)
        ktall[kv] = jnp.transpose(kall[kv].astype(F32)).astype(BF16)

    def scores(head, slot):
        s_ref, m_ref = slot[0], slot[4]
        s = nt(kall[head // GRP], q_v[:, head_lanes(head)])
        causal = lax.broadcasted_iota(jnp.int32, (half, half), 0) <= lax.broadcasted_iota(
            jnp.int32, (half, half), 1
        )
        s_p = s[:plen]
        s_l = jnp.where(causal, s[plen:top, :half], -jnp.inf)
        s_r = s[plen:top, half:]
        s_b = jnp.where(causal, s[top:, half:], -jnp.inf)
        s_ref[:plen] = s_p
        s_ref[plen:top, :half] = s_l
        s_ref[plen:top, half:] = s_r
        s_ref[top:, half:] = s_b
        m_p = jnp.max(s_p, axis=0, keepdims=True)
        m_l = jnp.max(s_l, axis=0, keepdims=True)
        m_r = jnp.max(jnp.maximum(s_r, s_b), axis=0, keepdims=True)
        m_ref[...] = jnp.maximum(m_p, jnp.concatenate([m_l, m_r], axis=1)) * to_exp2

    def value_products(head, slot):
        slot[1][...] = nt(vall[head // GRP], do_v[:, head_lanes(head)])

    def add_key_grad(head, slot):
        gk_acc[head // GRP] += nn(slot[3][...], q_v[:, head_lanes(head)])

    def add_value_grad(head, slot):
        gv_acc[head // GRP] += nn(slot[2][...], do_v[:, head_lanes(head)])

    def query_grad(head, slot):
        g_t = nn(ktall[head // GRP], slot[3][...]) * scaling
        gq_v[:, head_lanes(head)] = jnp.transpose(g_t).astype(BF16)

    quarter = half // 2

    def blocks(side):
        limit = top if side == 0 else keys
        return [(low, low + quarter) for low in range(0, limit, quarter)]

    def column(side):
        return slice(side * half, (side + 1) * half)

    def fold(x):
        return jnp.sum(x.reshape(-1, 8, half), axis=0)

    def exponentials(slot, side):
        s_ref, d_ref, m_ref = slot[0], slot[1], slot[4]
        cols = column(side)
        m = m_ref[:, cols]
        norm = jnp.zeros((8, half), F32)
        dots = jnp.zeros((8, half), F32)
        for low, high in blocks(side):
            e = jnp.exp2(s_ref[low:high, cols] * to_exp2 - m)
            s_ref[low:high, cols] = e
            norm = norm + fold(e)
            dots = dots + fold(e * d_ref[low:high, cols])
        inv = 1.0 / jnp.sum(norm, axis=0, keepdims=True)
        return inv, jnp.sum(dots, axis=0, keepdims=True) * inv

    def differences(slot, side, inv, dot_row):
        s_ref, d_ref, p_ref, ds_ref = slot[:4]
        cols = column(side)
        for low, high in blocks(side):
            p = s_ref[low:high, cols] * inv
            p_ref[low:high, cols] = p.astype(BF16)
            ds_ref[low:high, cols] = (p * (d_ref[low:high, cols] - dot_row)).astype(BF16)

    def step(head, cur, other):
        ahead = jnp.minimum(head + 1, heads - 1)
        behind = jnp.maximum(head - 1, 0)
        scores(ahead, other)
        stats_0 = exponentials(cur, 0)
        add_key_grad(behind, other)
        stats_1 = exponentials(cur, 1)
        add_value_grad(behind, other)
        differences(cur, 0, *stats_0)
        query_grad(behind, other)
        differences(cur, 1, *stats_1)
        value_products(ahead, other)

    def send_sums(kv):
        grad_k = gk_acc[kv] * scaling
        grad_v = gv_acc[kv]
        sa[kv, :, 0] = grad_k[:plen].astype(BF16).reshape(n_r, rows, HD)
        sa[kv, :, 1] = grad_v[:plen].astype(BF16).reshape(n_r, rows, HD)
        for i in range(1, n_r):
            sum_first(kv, row_peer(i), r).start()
        ra[kv, r] = sa[kv, r]
        lanes = head_lanes(kv)
        grk_ref[0, :, lanes] = grad_k[plen:].astype(BF16)
        grv_ref[0, :, lanes] = grad_v[plen:].astype(BF16)

    def store_queries(kv):
        cols = pl.ds(pl.multiple_of(kv * GRP * HD, HD), GRP * HD)
        return pltpu.make_async_copy(gq_v.at[:, cols], gq_out.at[0, :, cols], out_sem.at[kv])

    def combine(kv):
        for i in range(1, n_r):
            sum_first(kv, row_peer(i), row_peer(i)).wait_recv()
        sums = [jnp.zeros((2, rows, HD), F32) for _ in range(n_p)]
        for src in range(n_r):
            owner = prompt_of(src)
            term = ra[kv, src].astype(F32)
            for p in range(n_p):
                sums[p] = sums[p] + jnp.where(owner == p, term, 0.0)
        for p in range(n_p):
            kept[kv, p] = sums[p]
            sb[kv, p] = sums[p].astype(BF16)
        for i in range(1, n_p):
            sum_second(kv, column_peer(i), c).start()

    def finish(kv):
        lanes = head_lanes(kv)
        out = kept[kv, c]
        for i in range(1, n_p):
            sum_second(kv, column_peer(i), column_peer(i)).wait_recv()
            out = out + rb[kv, column_peer(i)].astype(F32)
        gpk_ref[0, :, lanes] = out[0]
        gpv_ref[0, :, lanes] = out[1]

    load_keys(0)
    if kv_heads > 1:
        send_second(1)
    scores(0, slots[0])
    value_products(0, slots[0])
    pairs = GRP // 2

    def pair(index, carry):
        kv = index // pairs
        place = index % pairs

        @pl.when((place == pairs - 1) & (kv < kv_heads - 1))
        def _():
            load_keys(kv + 1)

        @pl.when((place == 1) & (kv > 0))
        def _():
            send_sums(kv - 1)
            store_queries(kv - 1).start()

        @pl.when((place == 1) & (kv > 1))
        def _():
            combine(kv - 2)

        @pl.when((place == 2) & (kv < kv_heads - 2))
        def _():
            send_second(kv + 2)

        step(2 * index, slots[0], slots[1])
        step(2 * index + 1, slots[1], slots[0])
        return carry

    lax.fori_loop(0, heads // 2, pair, 0)
    add_key_grad(heads - 1, slots[1])
    add_value_grad(heads - 1, slots[1])
    send_sums(kv_heads - 1)
    query_grad(heads - 1, slots[1])
    store_queries(kv_heads - 1).start()
    if kv_heads > 1:
        combine(kv_heads - 2)
    for kv in range(kv_heads - 2):
        finish(kv)
    combine(kv_heads - 1)
    for kv in range(max(kv_heads - 2, 0), kv_heads):
        finish(kv)

    for kv in range(kv_heads):
        store_queries(kv).wait()
        for i in range(1, n_p):
            gather_first(kv, column_peer(i), c).wait_send()
        for i in range(1, n_r):
            gather_second(kv, row_peer(i), r).wait_send()
            sum_first(kv, row_peer(i), r).wait_send()
        for i in range(1, n_p):
            sum_second(kv, column_peer(i), c).wait_send()


def store_kernel(pieces, *refs):
    count = len(pieces)
    sources, targets, staged = refs[:count], refs[count : 2 * count], refs[2 * count : 3 * count]
    in_sem, out_sem = refs[3 * count :]
    loads, stores = [], []
    for k, parts in enumerate(pieces):
        size = sources[k].shape[1] // parts
        for part in range(parts):
            rows = pl.ds(part * size, size)
            place = len(loads)
            loads.append(
                pltpu.make_async_copy(
                    sources[k].at[:, rows], staged[k].at[:, rows], in_sem.at[place]
                )
            )
            stores.append(
                pltpu.make_async_copy(
                    staged[k].at[:, rows], targets[k].at[:, rows], out_sem.at[place]
                )
            )
    for load in loads:
        load.start()
    for load, store in zip(loads, stores):
        load.wait()
        store.start()
    for store in stores:
        store.wait()


def per_device(
    queries,
    resp_keys,
    resp_values,
    grad_out,
    prompt_keys,
    prompt_values,
    group_sizes,
    slot_response,
    lengths,
):
    n_p = lax.axis_size("prompt")
    n_r = lax.axis_size("resp")
    tok = queries.shape[1]
    width = queries.shape[2]
    rows = prompt_keys.shape[1]
    kv_width = prompt_keys.shape[2]
    kv_heads = kv_width // HD
    keys = rows * n_r + tok
    vmem = pl.BlockSpec(memory_space=pltpu.VMEM)
    hbm = pl.BlockSpec(memory_space=pltpu.HBM)
    anywhere = pl.BlockSpec(memory_space=pl.ANY)
    dma = pltpu.SemaphoreType.DMA
    out_shape = (
        jax.ShapeDtypeStruct(queries.shape, BF16),
        jax.ShapeDtypeStruct(resp_keys.shape, BF16),
        jax.ShapeDtypeStruct(resp_values.shape, BF16),
        jax.ShapeDtypeStruct(prompt_keys.shape, F32),
        jax.ShapeDtypeStruct(prompt_values.shape, F32),
    )
    results = pl.pallas_call(
        functools.partial(kernel, n_p, n_r),
        out_shape=out_shape,
        in_specs=[hbm] * 9,
        out_specs=(anywhere, vmem, vmem, vmem, vmem),
        scratch_shapes=[
            pltpu.VMEM((tok, width), BF16),
            pltpu.VMEM((tok, width), BF16),
            pltpu.VMEM((tok, width), BF16),
            pltpu.SMEM(group_sizes.shape, jnp.int32),
            pltpu.SMEM(slot_response.shape, jnp.int32),
            pltpu.SMEM(lengths.shape, jnp.int32),
            pltpu.VMEM((2, rows, kv_width), BF16),
            pltpu.VMEM((kv_heads, n_p, 2, rows, HD), BF16),
            pltpu.VMEM((kv_heads, n_r, 2, rows, HD), BF16),
            pltpu.VMEM((kv_heads, n_r, 2, rows, HD), BF16),
            pltpu.VMEM((kv_heads, n_r, 2, rows, HD), BF16),
            pltpu.VMEM((kv_heads, n_r, 2, rows, HD), BF16),
            pltpu.VMEM((kv_heads, n_p, 2, rows, HD), F32),
            pltpu.VMEM((kv_heads, n_p, 2, rows, HD), BF16),
            pltpu.VMEM((kv_heads, n_p, 2, rows, HD), BF16),
            pltpu.VMEM((kv_heads, keys, HD), BF16),
            pltpu.VMEM((kv_heads, keys, HD), BF16),
            pltpu.VMEM((kv_heads, HD, keys), BF16),
            pltpu.VMEM((kv_heads, keys, HD), F32),
            pltpu.VMEM((kv_heads, keys, HD), F32),
            pltpu.VMEM((keys, tok), F32),
            pltpu.VMEM((keys, tok), F32),
            pltpu.VMEM((keys, tok), F32),
            pltpu.VMEM((keys, tok), F32),
            pltpu.VMEM((keys, tok), BF16),
            pltpu.VMEM((keys, tok), BF16),
            pltpu.VMEM((keys, tok), BF16),
            pltpu.VMEM((keys, tok), BF16),
            pltpu.VMEM((1, tok), F32),
            pltpu.VMEM((1, tok), F32),
            dma((7,)),
            dma((2, kv_heads)),
            dma((kv_heads,)),
            dma((kv_heads, n_p)),
            dma((kv_heads, n_p)),
            dma((kv_heads, n_r)),
            dma((kv_heads, n_r)),
            dma((kv_heads, n_r)),
            dma((kv_heads, n_r)),
            dma((kv_heads, n_p)),
            dma((kv_heads, n_p)),
        ],
        compiler_params=pltpu.CompilerParams(
            collective_id=0, has_side_effects=True, vmem_limit_bytes=VMEM_LIMIT
        ),
        cost_estimate=pl.CostEstimate(
            flops=10 * tok * keys * width,
            bytes_accessed=4 * tok * width * 2,
            transcendentals=tok * keys * width // HD,
        ),
    )(
        queries,
        grad_out,
        resp_keys,
        resp_values,
        prompt_keys,
        prompt_values,
        group_sizes,
        slot_response,
        lengths,
    )
    pieces = (8, 2, 2, 1, 1)
    return pl.pallas_call(
        functools.partial(store_kernel, pieces),
        out_shape=out_shape,
        in_specs=[hbm] * len(out_shape),
        out_specs=(hbm,) * len(out_shape),
        scratch_shapes=[pltpu.VMEM(out.shape, out.dtype) for out in out_shape]
        + [dma((sum(pieces),)), dma((sum(pieces),))],
        compiler_params=pltpu.CompilerParams(vmem_limit_bytes=VMEM_LIMIT),
    )(*results)


def solution(mesh):
    in_specs = (
        P(("prompt", "resp"), None, None),
        P(("prompt", "resp"), None, None),
        P(("prompt", "resp"), None, None),
        P(("prompt", "resp"), None, None),
        P("prompt", "resp", None),
        P("prompt", "resp", None),
        P(),
        P(),
        P(("prompt", "resp")),
    )
    out_specs = (
        P(("prompt", "resp"), None, None),
        P(("prompt", "resp"), None, None),
        P(("prompt", "resp"), None, None),
        P("prompt", "resp", None),
        P("prompt", "resp", None),
    )
    return jax.shard_map(
        per_device, mesh=mesh, in_specs=in_specs, out_specs=out_specs, check_vma=False
    )
```

```python
import functools
import math

import jax
import jax.numpy as jnp
from jax import lax
from jax.experimental import pallas as pl
from jax.experimental.pallas import tpu as pltpu
from jax.sharding import PartitionSpec as P

HD = 128
GRP = 8
VMEM_LIMIT = 60 * 1024 * 1024
MESH = pl.DeviceIdType.MESH
F32 = jnp.float32
BF16 = jnp.bfloat16


def nt(a, b):
    return lax.dot_general(a, b, (((1,), (1,)), ((), ())), preferred_element_type=F32)


def nn(a, b):
    return jnp.dot(a, b, preferred_element_type=F32)


def kernel(
    n_p,
    n_r,
    q_hbm,
    do_hbm,
    rk_hbm,
    rv_hbm,
    pk_hbm,
    pv_hbm,
    sizes_hbm,
    slot_hbm,
    len_hbm,
    gq_out,
    grk_ref,
    grv_ref,
    gpk_ref,
    gpv_ref,
    q_v,
    do_v,
    gq_v,
    sizes_ref,
    slot_ref,
    len_ref,
    own,
    g1,
    s2,
    r2,
    sa,
    ra,
    sb,
    rb,
    kall,
    vall,
    ktall,
    gk_acc,
    gv_acc,
    s_0,
    s_1,
    d_0,
    d_1,
    p_0,
    p_1,
    ds_0,
    ds_1,
    m_0,
    m_1,
    in_sem,
    kv_sem,
    out_sem,
    g1_send,
    g1_recv,
    s2_send,
    s2_recv,
    a_send,
    a_recv,
    b_send,
    b_recv,
):
    c = lax.axis_index("prompt")
    r = lax.axis_index("resp")
    rows = g1.shape[3]
    kv_heads = kall.shape[0]
    heads = kv_heads * GRP
    tok = q_v.shape[0]
    plen = rows * n_r
    half = tok // 2
    top = plen + half
    keys = plen + tok
    scaling = 1.0 / math.sqrt(HD)
    to_exp2 = scaling * math.log2(math.e)

    def column_peer(i):
        return lax.rem(c + i, n_p)

    def row_peer(i):
        return lax.rem(r + i, n_r)

    def prompt_of(resp_index):
        value = slot_ref[c * n_r + resp_index]
        end = sizes_ref[0]
        found = (value >= end).astype(jnp.int32)
        for k in range(1, n_p - 1):
            end = end + sizes_ref[k]
            found = found + (value >= end).astype(jnp.int32)
        return found

    first = [
        pltpu.make_async_copy(pk_hbm.at[0], own.at[0], in_sem.at[0]),
        pltpu.make_async_copy(pv_hbm.at[0], own.at[1], in_sem.at[1]),
        pltpu.make_async_copy(sizes_hbm, sizes_ref, in_sem.at[2]),
        pltpu.make_async_copy(slot_hbm, slot_ref, in_sem.at[3]),
        pltpu.make_async_copy(len_hbm, len_ref, in_sem.at[4]),
    ]
    q_in = pltpu.make_async_copy(q_hbm.at[0], q_v, in_sem.at[5])
    do_in = pltpu.make_async_copy(do_hbm.at[0], do_v, in_sem.at[6])
    resp_in = []
    for kv in range(kv_heads):
        lanes = pl.ds(kv * HD, HD)
        resp_in.append(
            pltpu.make_async_copy(
                rk_hbm.at[0, :, lanes], kall.at[kv, pl.ds(plen, tok)], kv_sem.at[0, kv]
            )
        )
        resp_in.append(
            pltpu.make_async_copy(
                rv_hbm.at[0, :, lanes], vall.at[kv, pl.ds(plen, tok)], kv_sem.at[1, kv]
            )
        )
    for copy in first + [do_in, q_in] + resp_in:
        copy.start()

    barrier = pltpu.get_barrier_semaphore()
    for i in range(1, n_p):
        pl.semaphore_signal(barrier, inc=1, device_id=(column_peer(i), r), device_id_type=MESH)
    for i in range(1, n_r):
        pl.semaphore_signal(barrier, inc=1, device_id=(c, row_peer(i)), device_id_type=MESH)
    for copy in first:
        copy.wait()
    for kv in range(kv_heads):
        g1[kv, c] = own[:, :, kv * HD : (kv + 1) * HD]
    pl.semaphore_wait(barrier, n_p + n_r - 2)

    def gather_first(kv, to, slot):
        return pltpu.make_async_remote_copy(
            src_ref=g1.at[kv, slot],
            dst_ref=g1.at[kv, slot],
            send_sem=g1_send.at[kv, to],
            recv_sem=g1_recv.at[kv, slot],
            device_id=(to, r),
            device_id_type=MESH,
        )

    def gather_second(kv, to, slot):
        return pltpu.make_async_remote_copy(
            src_ref=s2.at[kv, to],
            dst_ref=r2.at[kv, slot],
            send_sem=s2_send.at[kv, to],
            recv_sem=s2_recv.at[kv, slot],
            device_id=(c, to),
            device_id_type=MESH,
        )

    def sum_first(kv, to, slot):
        return pltpu.make_async_remote_copy(
            src_ref=sa.at[kv, to],
            dst_ref=ra.at[kv, slot],
            send_sem=a_send.at[kv, to],
            recv_sem=a_recv.at[kv, slot],
            device_id=(c, to),
            device_id_type=MESH,
        )

    def sum_second(kv, to, slot):
        return pltpu.make_async_remote_copy(
            src_ref=sb.at[kv, to],
            dst_ref=rb.at[kv, slot],
            send_sem=b_send.at[kv, to],
            recv_sem=b_recv.at[kv, slot],
            device_id=(to, r),
            device_id_type=MESH,
        )

    def send_first(kv):
        for i in range(1, n_p):
            gather_first(kv, column_peer(i), c).start()

    def picked(kv, to):
        owner = prompt_of(to)
        block = g1[kv, 0]
        for p in range(1, n_p):
            block = jnp.where(owner == p, g1[kv, p], block)
        return block

    def send_second(kv):
        for i in range(1, n_p):
            gather_first(kv, column_peer(i), column_peer(i)).wait_recv()
        for i in range(1, n_r):
            to = row_peer(i)
            s2[kv, to] = picked(kv, to)
            gather_second(kv, to, r).start()
        r2[kv, r] = picked(kv, r)

    send_first(0)
    send_second(0)
    for kv in range(1, kv_heads):
        send_first(kv)
    gk_acc[...] = jnp.zeros_like(gk_acc)
    gv_acc[...] = jnp.zeros_like(gv_acc)
    for ref in (p_0, p_1, ds_0, ds_1):
        ref[...] = jnp.zeros_like(ref)
    do_in.wait()
    live_mask = lax.broadcasted_iota(jnp.int32, (tok, HD), 0) < len_ref[0]

    def mask_rows(head, carry):
        lanes = pl.ds(pl.multiple_of(head * HD, HD), HD)
        do_v[:, lanes] = jnp.where(live_mask, do_v[:, lanes], jnp.zeros((), BF16))
        return carry

    lax.fori_loop(0, heads, mask_rows, 0)
    q_in.wait()
    for copy in resp_in:
        copy.wait()

    slots = ((s_0, d_0, p_0, ds_0, m_0), (s_1, d_1, p_1, ds_1, m_1))

    def head_lanes(head):
        return pl.ds(pl.multiple_of(head * HD, HD), HD)

    def load_keys(kv):
        for i in range(1, n_r):
            gather_second(kv, row_peer(i), row_peer(i)).wait_recv()
        kall[kv, :plen] = r2[kv, :, 0].reshape(plen, HD)
        vall[kv, :plen] = r2[kv, :, 1].reshape(plen, HD)
        ktall[kv] = jnp.transpose(kall[kv].astype(F32)).astype(BF16)

    def scores(head, slot):
        s_ref, m_ref = slot[0], slot[4]
        s = nt(kall[head // GRP], q_v[:, head_lanes(head)])
        causal = lax.broadcasted_iota(jnp.int32, (half, half), 0) <= lax.broadcasted_iota(
            jnp.int32, (half, half), 1
        )
        s_p = s[:plen]
        s_l = jnp.where(causal, s[plen:top, :half], -jnp.inf)
        s_r = s[plen:top, half:]
        s_b = jnp.where(causal, s[top:, half:], -jnp.inf)
        s_ref[:plen] = s_p
        s_ref[plen:top, :half] = s_l
        s_ref[plen:top, half:] = s_r
        s_ref[top:, half:] = s_b
        m_p = jnp.max(s_p, axis=0, keepdims=True)
        m_l = jnp.max(s_l, axis=0, keepdims=True)
        m_r = jnp.max(jnp.maximum(s_r, s_b), axis=0, keepdims=True)
        m_ref[...] = jnp.maximum(m_p, jnp.concatenate([m_l, m_r], axis=1)) * to_exp2

    def value_products(head, slot):
        slot[1][...] = nt(vall[head // GRP], do_v[:, head_lanes(head)])

    def add_key_grad(head, slot):
        gk_acc[head // GRP] += nn(slot[3][...], q_v[:, head_lanes(head)])

    def add_value_grad(head, slot):
        gv_acc[head // GRP] += nn(slot[2][...], do_v[:, head_lanes(head)])

    def query_grad(head, slot):
        g_t = nn(ktall[head // GRP], slot[3][...]) * scaling
        gq_v[:, head_lanes(head)] = jnp.transpose(g_t).astype(BF16)

    quarter = half // 2

    def blocks(side):
        limit = top if side == 0 else keys
        return [(low, low + quarter) for low in range(0, limit, quarter)]

    def column(side):
        return slice(side * half, (side + 1) * half)

    def fold(x):
        return jnp.sum(x.reshape(-1, 8, half), axis=0)

    def exponentials(slot, side):
        s_ref, d_ref, m_ref = slot[0], slot[1], slot[4]
        cols = column(side)
        m = m_ref[:, cols]
        norm = jnp.zeros((8, half), F32)
        dots = jnp.zeros((8, half), F32)
        for low, high in blocks(side):
            e = jnp.exp2(s_ref[low:high, cols] * to_exp2 - m)
            s_ref[low:high, cols] = e
            norm = norm + fold(e)
            dots = dots + fold(e * d_ref[low:high, cols])
        inv = 1.0 / jnp.sum(norm, axis=0, keepdims=True)
        return inv, jnp.sum(dots, axis=0, keepdims=True) * inv

    def differences(slot, side, inv, dot_row):
        s_ref, d_ref, p_ref, ds_ref = slot[:4]
        cols = column(side)
        for low, high in blocks(side):
            p = s_ref[low:high, cols] * inv
            p_ref[low:high, cols] = p.astype(BF16)
            ds_ref[low:high, cols] = (p * (d_ref[low:high, cols] - dot_row)).astype(BF16)

    def step(head, cur, other):
        ahead = jnp.minimum(head + 1, heads - 1)
        behind = jnp.maximum(head - 1, 0)
        scores(ahead, other)
        stats_0 = exponentials(cur, 0)
        add_key_grad(behind, other)
        stats_1 = exponentials(cur, 1)
        add_value_grad(behind, other)
        differences(cur, 0, *stats_0)
        query_grad(behind, other)
        differences(cur, 1, *stats_1)
        value_products(ahead, other)

    def send_sums(kv):
        grad_k = gk_acc[kv] * scaling
        grad_v = gv_acc[kv]
        sa[kv, :, 0] = grad_k[:plen].astype(BF16).reshape(n_r, rows, HD)
        sa[kv, :, 1] = grad_v[:plen].astype(BF16).reshape(n_r, rows, HD)
        for i in range(1, n_r):
            sum_first(kv, row_peer(i), r).start()
        ra[kv, r] = sa[kv, r]
        lanes = head_lanes(kv)
        grk_ref[0, :, lanes] = grad_k[plen:].astype(BF16)
        grv_ref[0, :, lanes] = grad_v[plen:].astype(BF16)
        store_queries(kv).start()

    def store_queries(kv):
        cols = pl.ds(pl.multiple_of(kv * GRP * HD, HD), GRP * HD)
        return pltpu.make_async_copy(gq_v.at[:, cols], gq_out.at[0, :, cols], out_sem.at[kv])

    def combine(kv):
        for i in range(1, n_r):
            sum_first(kv, row_peer(i), row_peer(i)).wait_recv()
        sums = [jnp.zeros((2, rows, HD), F32) for _ in range(n_p)]
        for src in range(n_r):
            owner = prompt_of(src)
            term = ra[kv, src].astype(F32)
            for p in range(n_p):
                sums[p] = sums[p] + jnp.where(owner == p, term, 0.0)
        for p in range(n_p):
            sb[kv, p] = sums[p]
        for i in range(1, n_p):
            sum_second(kv, column_peer(i), c).start()

    def finish(kv):
        lanes = head_lanes(kv)
        out = sb[kv, c]
        for i in range(1, n_p):
            sum_second(kv, column_peer(i), column_peer(i)).wait_recv()
            out = out + rb[kv, column_peer(i)]
        gpk_ref[0, :, lanes] = out[0]
        gpv_ref[0, :, lanes] = out[1]

    if kv_heads > 1:
        send_second(1)
    load_keys(0)
    scores(0, slots[0])
    value_products(0, slots[0])
    pairs = GRP // 2

    def pair(index, carry):
        kv = index // pairs
        place = index % pairs

        @pl.when((place == pairs - 1) & (kv < kv_heads - 1))
        def _():
            load_keys(kv + 1)

        @pl.when((place == 1) & (kv > 0))
        def _():
            send_sums(kv - 1)

        @pl.when((place == 1) & (kv > 1))
        def _():
            combine(kv - 2)

        @pl.when((place == 2) & (kv < kv_heads - 2))
        def _():
            send_second(kv + 2)

        step(2 * index, slots[0], slots[1])
        step(2 * index + 1, slots[1], slots[0])
        return carry

    lax.fori_loop(0, heads // 2, pair, 0)
    add_key_grad(heads - 1, slots[1])
    add_value_grad(heads - 1, slots[1])
    query_grad(heads - 1, slots[1])
    send_sums(kv_heads - 1)
    if kv_heads > 1:
        combine(kv_heads - 2)
    for kv in range(kv_heads - 2):
        finish(kv)
    combine(kv_heads - 1)
    for kv in range(max(kv_heads - 2, 0), kv_heads):
        finish(kv)

    for kv in range(kv_heads):
        store_queries(kv).wait()
        for i in range(1, n_p):
            gather_first(kv, column_peer(i), c).wait_send()
        for i in range(1, n_r):
            gather_second(kv, row_peer(i), r).wait_send()
            sum_first(kv, row_peer(i), r).wait_send()
        for i in range(1, n_p):
            sum_second(kv, column_peer(i), c).wait_send()


def store_kernel(pieces, *refs):
    count = len(pieces)
    sources, targets, staged = refs[:count], refs[count : 2 * count], refs[2 * count : 3 * count]
    in_sem, out_sem = refs[3 * count :]
    loads, stores = [], []
    for k, parts in enumerate(pieces):
        size = sources[k].shape[1] // parts
        for part in range(parts):
            rows = pl.ds(part * size, size)
            place = len(loads)
            loads.append(
                pltpu.make_async_copy(
                    sources[k].at[:, rows], staged[k].at[:, rows], in_sem.at[place]
                )
            )
            stores.append(
                pltpu.make_async_copy(
                    staged[k].at[:, rows], targets[k].at[:, rows], out_sem.at[place]
                )
            )
    for load in loads:
        load.start()
    for load, store in zip(loads, stores):
        load.wait()
        store.start()
    for store in stores:
        store.wait()


def per_device(
    queries,
    resp_keys,
    resp_values,
    grad_out,
    prompt_keys,
    prompt_values,
    group_sizes,
    slot_response,
    lengths,
):
    n_p = lax.axis_size("prompt")
    n_r = lax.axis_size("resp")
    tok = queries.shape[1]
    width = queries.shape[2]
    rows = prompt_keys.shape[1]
    kv_width = prompt_keys.shape[2]
    kv_heads = kv_width // HD
    keys = rows * n_r + tok
    vmem = pl.BlockSpec(memory_space=pltpu.VMEM)
    hbm = pl.BlockSpec(memory_space=pltpu.HBM)
    anywhere = pl.BlockSpec(memory_space=pl.ANY)
    dma = pltpu.SemaphoreType.DMA
    out_shape = (
        jax.ShapeDtypeStruct(queries.shape, BF16),
        jax.ShapeDtypeStruct(resp_keys.shape, BF16),
        jax.ShapeDtypeStruct(resp_values.shape, BF16),
        jax.ShapeDtypeStruct(prompt_keys.shape, F32),
        jax.ShapeDtypeStruct(prompt_values.shape, F32),
    )
    results = pl.pallas_call(
        functools.partial(kernel, n_p, n_r),
        out_shape=out_shape,
        in_specs=[hbm] * 9,
        out_specs=(anywhere, vmem, vmem, vmem, vmem),
        scratch_shapes=[
            pltpu.VMEM((tok, width), BF16),
            pltpu.VMEM((tok, width), BF16),
            pltpu.VMEM((tok, width), BF16),
            pltpu.SMEM(group_sizes.shape, jnp.int32),
            pltpu.SMEM(slot_response.shape, jnp.int32),
            pltpu.SMEM(lengths.shape, jnp.int32),
            pltpu.VMEM((2, rows, kv_width), BF16),
            pltpu.VMEM((kv_heads, n_p, 2, rows, HD), BF16),
            pltpu.VMEM((kv_heads, n_r, 2, rows, HD), BF16),
            pltpu.VMEM((kv_heads, n_r, 2, rows, HD), BF16),
            pltpu.VMEM((kv_heads, n_r, 2, rows, HD), BF16),
            pltpu.VMEM((kv_heads, n_r, 2, rows, HD), BF16),
            pltpu.VMEM((kv_heads, n_p, 2, rows, HD), F32),
            pltpu.VMEM((kv_heads, n_p, 2, rows, HD), F32),
            pltpu.VMEM((kv_heads, keys, HD), BF16),
            pltpu.VMEM((kv_heads, keys, HD), BF16),
            pltpu.VMEM((kv_heads, HD, keys), BF16),
            pltpu.VMEM((kv_heads, keys, HD), F32),
            pltpu.VMEM((kv_heads, keys, HD), F32),
            pltpu.VMEM((keys, tok), F32),
            pltpu.VMEM((keys, tok), F32),
            pltpu.VMEM((keys, tok), F32),
            pltpu.VMEM((keys, tok), F32),
            pltpu.VMEM((keys, tok), BF16),
            pltpu.VMEM((keys, tok), BF16),
            pltpu.VMEM((keys, tok), BF16),
            pltpu.VMEM((keys, tok), BF16),
            pltpu.VMEM((1, tok), F32),
            pltpu.VMEM((1, tok), F32),
            dma((7,)),
            dma((2, kv_heads)),
            dma((kv_heads,)),
            dma((kv_heads, n_p)),
            dma((kv_heads, n_p)),
            dma((kv_heads, n_r)),
            dma((kv_heads, n_r)),
            dma((kv_heads, n_r)),
            dma((kv_heads, n_r)),
            dma((kv_heads, n_p)),
            dma((kv_heads, n_p)),
        ],
        compiler_params=pltpu.CompilerParams(
            collective_id=0, has_side_effects=True, vmem_limit_bytes=VMEM_LIMIT
        ),
        cost_estimate=pl.CostEstimate(
            flops=10 * tok * keys * width,
            bytes_accessed=4 * tok * width * 2,
            transcendentals=tok * keys * width // HD,
        ),
    )(
        queries,
        grad_out,
        resp_keys,
        resp_values,
        prompt_keys,
        prompt_values,
        group_sizes,
        slot_response,
        lengths,
    )
    pieces = (4, 1, 1, 1, 1)
    return pl.pallas_call(
        functools.partial(store_kernel, pieces),
        out_shape=out_shape,
        in_specs=[hbm] * len(out_shape),
        out_specs=(hbm,) * len(out_shape),
        scratch_shapes=[pltpu.VMEM(out.shape, out.dtype) for out in out_shape]
        + [dma((sum(pieces),)), dma((sum(pieces),))],
        compiler_params=pltpu.CompilerParams(vmem_limit_bytes=VMEM_LIMIT),
    )(*results)


def solution(mesh):
    in_specs = (
        P(("prompt", "resp"), None, None),
        P(("prompt", "resp"), None, None),
        P(("prompt", "resp"), None, None),
        P(("prompt", "resp"), None, None),
        P("prompt", "resp", None),
        P("prompt", "resp", None),
        P(),
        P(),
        P(("prompt", "resp")),
    )
    out_specs = (
        P(("prompt", "resp"), None, None),
        P(("prompt", "resp"), None, None),
        P(("prompt", "resp"), None, None),
        P("prompt", "resp", None),
        P("prompt", "resp", None),
    )
    return jax.shard_map(
        per_device, mesh=mesh, in_specs=in_specs, out_specs=out_specs, check_vma=False
    )
```
